512 devices in a mesh: grp: 2 (over z_hi), seq: 32 (over y, x, core), dp: 8 (over z_lo).
Axes of the slice: x: 4, y: 4, z: 16 (z_hi: 2, z_lo: 8; z = z_hi * 8 + z_lo), core: 2. Of those that a mesh axis runs over, the one named last changes fastest.
Arguments:
- queries: bfloat16 [8, 4096, 4096], P('dp', 'seq'), may hold values from -130 to 130
- keys: bfloat16 [8, 4096, 4096], P('dp', 'seq'), may hold values from -8 to 8
- values: bfloat16 [8, 4096, 4096], P('dp', 'seq', 'grp'), may hold values from -6 to 6
- cotangent: bfloat16 [8, 4096, 4096], P('dp', 'seq', 'grp'), may hold values from -0.078125 to 0.078125
- captions: bfloat16 [8, 512, 4096], P('dp', 'seq'), may hold values from -6 to 6
- caption_len: int32 [8], P('dp'), may hold values from 1 to 512, 2560 in all
- proj_weight: bfloat16 [4096, 8192], P('dp', 'seq'), may hold values from -0.09375 to 0.09375
Outputs:
- attended: bfloat16 [8, 4096, 4096], P('dp', 'seq', 'grp')
- proj_grad: float32 [4096, 8192], P('dp', 'seq')
The draws below stay inside these ranges and needn't reach their ends.
Inputs may be any that keep to these rules, and one draw needn't show every extreme that they name: `caption_len`: each caption has at least one token; some caption has all 512.
All inputs are finite; a program needn't handle non-finite values. No bound on the sum of `caption_len` on one device may be relied on, other than what follows from the above.
Results may differ from the reference program's by a relative error of at most 0.0085.
The reference program's roundings to bfloat16 on the way (of `normed`, `text_kv`, `grad_scores` and `kv_grad`) count: a program that leaves them out, or rounds other values in their place, can miss the bound.
Values may be sent and summed in bfloat16 or wider, within the bound.
No kernel may reach another device: no remote copies, remote signals or barrier semaphores. Data moves between devices by JAX's collectives and lax.ppermute only.
A program may use at most 128 MiB of HBM per device.

```python
import math
import jax
import jax.numpy as jnp
import numpy as np
from jax import lax

HD = 128
TD = 4096
TXT = 512
HEADS = 32
HH = 4096
SEQLEN = 4096
SAMPLES = 8
N_DP = 8


def paired(key):
    shape = (SAMPLES, SEQLEN, HH)
    base_keys = jnp.clip(jax.random.normal(jax.random.fold_in(key, 11), shape, jnp.float32), -6.0, 6.0)
    base_queries = 2.5 * jnp.clip(jax.random.normal(jax.random.fold_in(key, 12), shape, jnp.float32), -6.0, 6.0)
    keys_out = base_keys
    queries_out = base_queries
    return (queries_out, keys_out)


def draw_queries(key, part):
    queries_out, keys_out = paired(key)
    return queries_out.astype(jnp.bfloat16)


def draw_keys(key, part):
    queries_out, keys_out = paired(key)
    return keys_out.astype(jnp.bfloat16)


def level_of(own_key, extent, cuts, smallest, top_value):
    def one(dim, blocks):
        steps = jax.random.uniform(jax.random.fold_in(jax.random.fold_in(own_key, 6), dim), (blocks,), jnp.float32, smallest / len(cuts), top_value / len(cuts))
        return jnp.repeat(jnp.exp(steps), extent[dim] // blocks).reshape((-1,) + (1,) * (len(extent) - dim - 1))

    loudness = one(*cuts[0])
    for cut in cuts[1:]:
        loudness = loudness * one(*cut)
    return loudness


def profile(amount, total, limit, skew):
    weights = [(1 << 20) // math.isqrt(grade ** skew) + 1 for grade in range(2, amount + 1)]
    rest, given = total - limit - (amount - 1), [1] * (amount - 1)
    while rest > 0:
        movable = [i for i in range(amount - 1) if given[i] < limit]
        mass, budget = sum([weights[i] for i in movable]), rest
        for i in movable:
            extra = min(limit - given[i], max(1, budget * weights[i] // mass), rest)
            given[i] = given[i] + extra
            rest = rest - extra
    return np.array([limit] + given)


def uneven(key, number_of, total, bound, lean):
    if number_of == 2:
        one = jax.random.randint(key, (), max(1, total - bound), min(bound, total - 1) + 1)
        return jnp.stack([one, total - one])
    lengths = jnp.asarray(profile(number_of, total, bound, lean), jnp.int32)
    couples = (number_of - 1) // 2
    giver, sink = lengths[1:1 + 2 * couples:2], lengths[2:2 + 2 * couples:2]
    room = jnp.minimum(giver - 1, bound - sink)
    moved = jax.random.randint(jax.random.fold_in(key, 1), (couples,), 0, 1 << 20) % (room + 1)
    lengths = lengths.at[1:1 + 2 * couples:2].set(giver - moved).at[2:2 + 2 * couples:2].set(sink + moved)
    return lengths[jax.random.permutation(jax.random.fold_in(key, 2), number_of)]


def centred(key, shape, scale, bound, split=(), kind=jnp.bfloat16):
    values = jax.random.normal(key, shape, jnp.float32) * scale
    if len(split) > 0:
        values = level_of(key, shape, split, -0.22, 0.18) * values
    return jnp.clip(values, min=-bound, max=bound).astype(kind)


def setup_inputs(seed: int = 0) -> dict:
    arg_keys = jax.random.split(jax.random.key(seed), 8)
    return {
        "queries": draw_queries(jax.random.fold_in(arg_keys[7], 71), 0),
        "keys": draw_keys(jax.random.fold_in(arg_keys[7], 71), 0),
        "values": centred(arg_keys[2], (SAMPLES, SEQLEN, HH), 1.0, 6.0, ((0, 8), (1, 32), (2, 2))),
        "cotangent": centred(arg_keys[3], (SAMPLES, SEQLEN, HH), (1.0 / (SEQLEN * N_DP) ** 0.5), 0.078125, ((0, 8), (1, 32), (2, 2))),
        "captions": centred(arg_keys[4], (SAMPLES, TXT, TD), 1.0, 6.0, ((0, 8), (1, 32))),
        "caption_len": uneven(arg_keys[5], SAMPLES, N_DP * TXT * 5 // 8, TXT, 0).astype(jnp.int32),
        "proj_weight": centred(arg_keys[6], (TD, 2 * HH), TD ** -0.5, 0.09375, ((0, 8), (1, 32))),
    }


def normalize(rows):
    wide = rows.astype(jnp.float32)
    square = lax.optimization_barrier(jnp.mean(wide * wide, axis=-1, keepdims=True))
    return (wide * lax.rsqrt(square + 1e-06)).astype(jnp.bfloat16)

def softmax_rows(scores):
    top = lax.optimization_barrier(jnp.max(scores, axis=-1, keepdims=True))
    expo = jnp.exp(scores - top)
    return expo / lax.optimization_barrier(jnp.sum(expo, axis=-1, keepdims=True))

def self_pass(q_head, k_head, v_head):
    score_scale = 1.0 / math.sqrt(HD)
    scores = lax.dot_general(q_head, k_head, (((1,), (1,)), ((), ())), preferred_element_type=jnp.float32) * score_scale
    soft = softmax_rows(scores)
    return jnp.dot(soft.astype(jnp.bfloat16), v_head, preferred_element_type=jnp.float32)

def cross_pass(q_head, text_kv, cot_head, length):
    score_scale = 1.0 / math.sqrt(HD)
    text_keys = text_kv[:, :HD]
    text_vals = text_kv[:, HD:]
    scores = lax.dot_general(q_head, text_keys, (((1,), (1,)), ((), ())), preferred_element_type=jnp.float32) * score_scale
    live_keys = jnp.arange(text_kv.shape[0], dtype=jnp.int32) < length.astype(jnp.int32)
    scores = jnp.where(live_keys[None, :], scores, -jnp.inf)
    soft = softmax_rows(scores)
    soft_low = soft.astype(jnp.bfloat16)
    cross_out = jnp.dot(soft_low, text_vals, preferred_element_type=jnp.float32)
    back_soft = lax.dot_general(cot_head, text_vals, (((1,), (1,)), ((), ())), preferred_element_type=jnp.float32)
    grad_vals = lax.dot_general(soft_low, cot_head, (((0,), (0,)), ((), ())), preferred_element_type=jnp.float32)
    inner = lax.optimization_barrier(jnp.sum(soft * back_soft, axis=-1, keepdims=True))
    grad_scores = (soft * (back_soft - inner) * score_scale).astype(jnp.bfloat16)
    grad_keys = lax.dot_general(grad_scores, q_head, (((0,), (0,)), ((), ())), preferred_element_type=jnp.float32)
    kv_grad = jnp.concatenate([grad_keys, grad_vals], axis=1).astype(jnp.bfloat16)
    return (cross_out, kv_grad)

def split_heads(array):
    return array.reshape(SAMPLES, SEQLEN, HEADS, HD).transpose(0, 2, 1, 3)

def reference(queries, keys, values, cotangent, captions, caption_len, proj_weight):
    normed = normalize(captions)
    text_kv = jnp.einsum('std,dc->stc', normed.astype(jnp.float32), proj_weight.astype(jnp.float32)).astype(jnp.bfloat16)
    text_kv = text_kv.reshape(SAMPLES, TXT, HEADS, 2 * HD).transpose(0, 2, 1, 3)

    def one_sample(items):
        q_all, k_all, v_all, c_all, kv_all, length = items

        def one_head(parts):
            q_head, k_head, v_head, c_head, kv_head = parts
            self_out = self_pass(q_head, k_head, v_head)
            cross_out, kv_grad = cross_pass(q_head, kv_head, c_head, length)
            return ((self_out + cross_out).astype(jnp.bfloat16), kv_grad)
        return lax.map(one_head, (q_all, k_all, v_all, c_all, kv_all))
    outputs, grads = lax.map(one_sample, (split_heads(queries), split_heads(keys), split_heads(values), split_heads(cotangent), text_kv, caption_len))
    attended = outputs.transpose(0, 2, 1, 3).reshape(SAMPLES, SEQLEN, HH)
    grads = grads.transpose(0, 2, 1, 3).reshape(SAMPLES, TXT, 2 * HH)
    proj_grad = jnp.einsum('std,stc->dc', normed.astype(jnp.float32), grads.astype(jnp.float32))
    return (attended, proj_grad)
```

```python
import math

import jax
import jax.numpy as jnp
from jax import lax
from jax.experimental import pallas as pl
from jax.experimental.pallas import tpu as pltpu
from jax.sharding import Mesh
from jax.sharding import PartitionSpec as P

HD = 128
SCALE = 1.0 / math.sqrt(HD)
LOG2E = math.log2(math.e)
PLANE = ("y", "x", "c")
CHIPS = ("y", "x")
RING = ("g", "d")
NT = (((1,), (1,)), ((), ()))
TN = (((0,), (0,)), ((), ()))
VMEM = 48 * 1024 * 1024
SWAP = [(0, 1), (1, 0)]


def normalize(rows):
    wide = rows.astype(jnp.float32)
    square = jnp.mean(wide * wide, axis=-1, keepdims=True)
    return (wide * lax.rsqrt(square + 1e-06)).astype(jnp.bfloat16)


def pack_kernel(side_ref, wide_ref, half_ref, out_ref):
    rows = out_ref.shape[2]
    for dest in range(out_ref.shape[0]):
        head, part = dest // 2, dest % 2
        for slot, ref in enumerate((wide_ref, half_ref)):
            out_ref[dest, slot] = ref[0, part * rows : (part + 1) * rows, head * HD : (head + 1) * HD]


def pack(side, wide, half):
    _, rows, width = half.shape
    dests = 2 * width // HD
    return pl.pallas_call(
        pack_kernel,
        grid_spec=pltpu.PrefetchScalarGridSpec(
            num_scalar_prefetch=1,
            grid=(1,),
            in_specs=[
                pl.BlockSpec((1, rows, width), lambda j, side_ref: (0, 0, side_ref[0])),
                pl.BlockSpec((1, rows, width), lambda j, side_ref: (0, 0, 0)),
            ],
            out_specs=pl.BlockSpec((dests, 2, rows // 2, HD), lambda j, side_ref: (0, 0, 0, 0)),
        ),
        out_shape=jax.ShapeDtypeStruct((dests, 2, rows // 2, HD), half.dtype),
        compiler_params=pltpu.CompilerParams(vmem_limit_bytes=VMEM),
        cost_estimate=pl.CostEstimate(flops=0, bytes_accessed=4 * rows * width * 2, transcendentals=0),
        name="pack",
    )(side, wide, half)


def unpack_kernel(in_ref, out_ref):
    rows = in_ref.shape[1]
    for source in range(in_ref.shape[0]):
        head, part = source // 2, source % 2
        out_ref[0, part * rows : (part + 1) * rows, head * HD : (head + 1) * HD] = in_ref[source]


def unpack(pieces):
    sources, rows, _ = pieces.shape
    width = sources // 2 * HD
    return pl.pallas_call(
        unpack_kernel,
        out_shape=jax.ShapeDtypeStruct((1, 2 * rows, width), pieces.dtype),
        compiler_params=pltpu.CompilerParams(vmem_limit_bytes=VMEM),
        cost_estimate=pl.CostEstimate(flops=0, bytes_accessed=8 * rows * width, transcendentals=0),
        name="unpack",
    )(pieces)


def project_kernel(spot_ref, rows_ref, own_ref, taken_ref, other_ref, out_ref):
    here, core = spot_ref[0], spot_ref[1]
    reach, depth, _ = taken_ref.shape
    n_dp = rows_ref.shape[1] // depth

    def part(block, weight):
        columns = pl.ds(pl.multiple_of(lax.rem(block + 2 * n_dp, n_dp) * depth, depth), depth)
        return jnp.dot(rows_ref[:, columns], weight, preferred_element_type=jnp.float32)

    way = 1 - 2 * core
    total = part(here, own_ref[...])
    for t in range(1, reach):
        total += part(here - way * t, taken_ref[t - 1])
        total += part(here + way * t, other_ref[t - 1])
    last = jnp.where(core == 0, taken_ref[reach - 1], other_ref[reach - 1])
    total += part(here - reach, last)
    out_ref[...] = total.astype(out_ref.dtype)


def project(spot, rows, own, taken, other):
    vmem = pl.BlockSpec(memory_space=pltpu.VMEM)
    return pl.pallas_call(
        project_kernel,
        in_specs=[pl.BlockSpec(memory_space=pltpu.SMEM), vmem, vmem, vmem, vmem],
        out_specs=vmem,
        out_shape=jax.ShapeDtypeStruct((rows.shape[0], own.shape[1]), jnp.bfloat16),
        compiler_params=pltpu.CompilerParams(vmem_limit_bytes=VMEM),
        cost_estimate=pl.CostEstimate(
            flops=2 * rows.size * own.shape[1], bytes_accessed=2 * (rows.size + 2 * taken.size), transcendentals=0
        ),
        name="project",
    )(spot, rows, own, taken, other)


def cross_kernel(length_ref, q_ref, c_ref, kv_ref, out_ref, grad_ref):
    step = pl.program_id(0)
    block = out_ref.shape[0]
    tokens = kv_ref.shape[0]
    q = q_ref[:, 0].reshape(block, HD)
    cot = c_ref[:, 0].reshape(block, HD)
    text_keys = kv_ref[:, :HD]
    text_vals = kv_ref[:, HD:]
    place = lax.broadcasted_iota(jnp.int32, (tokens, 1), 0)
    half = tokens // 2
    part = jnp.where(place >= half, 1, 0)
    inside = place - part * half
    token = (inside >> 4) * 32 + part * 16 + (inside & 15)
    live = token < length_ref[0]
    scores = lax.dot_general(text_keys, q, NT, preferred_element_type=jnp.float32) * SCALE
    scores = jnp.where(live, scores, -jnp.inf)
    top = jnp.max(scores, axis=0, keepdims=True)
    expo = jnp.exp(scores - top)
    soft = expo / jnp.sum(expo, axis=0, keepdims=True)
    soft_low = soft.astype(jnp.bfloat16)
    out_t = lax.dot_general(text_vals, soft_low, TN, preferred_element_type=jnp.float32)
    out_ref[...] = out_t.T
    back = lax.dot_general(text_vals, cot, NT, preferred_element_type=jnp.float32)
    inner = jnp.sum(soft * back, axis=0, keepdims=True)
    grad_scores = (soft * (back - inner) * SCALE).astype(jnp.bfloat16)
    grad_keys = jnp.dot(grad_scores, q, preferred_element_type=jnp.float32)
    grad_vals = jnp.dot(soft_low, cot, preferred_element_type=jnp.float32)

    @pl.when(step == 0)
    def _():
        grad_ref[:, :HD] = grad_keys
        grad_ref[:, HD:] = grad_vals

    @pl.when(step > 0)
    def _():
        grad_ref[:, :HD] += grad_keys
        grad_ref[:, HD:] += grad_vals


def cross_attend(length, q_cot, text_kv, blocks=4):
    sources, _, rows, _ = q_cot.shape
    queries = sources * rows
    tokens = text_kv.shape[0]
    return pl.pallas_call(
        cross_kernel,
        grid_spec=pltpu.PrefetchScalarGridSpec(
            num_scalar_prefetch=1,
            grid=(blocks,),
            in_specs=[
                pl.BlockSpec((sources // blocks, 1, rows, HD), lambda j, n: (j, 0, 0, 0)),
                pl.BlockSpec((sources // blocks, 1, rows, HD), lambda j, n: (j, 1, 0, 0)),
                pl.BlockSpec((tokens, 2 * HD), lambda j, n: (0, 0)),
            ],
            out_specs=[
                pl.BlockSpec((queries // blocks, HD), lambda j, n: (j, 0)),
                pl.BlockSpec((tokens, 2 * HD), lambda j, n: (0, 0)),
            ],
        ),
        out_shape=[
            jax.ShapeDtypeStruct((queries, HD), jnp.float32),
            jax.ShapeDtypeStruct((tokens, 2 * HD), jnp.float32),
        ],
        compiler_params=pltpu.CompilerParams(vmem_limit_bytes=VMEM),
        cost_estimate=pl.CostEstimate(
            flops=10 * queries * tokens * HD, bytes_accessed=3 * 1024 * 1024, transcendentals=queries * tokens
        ),
        name="cross",
    )(length, q_cot, q_cot, text_kv)


def self_kernel(q_ref, near_ref, far_ref, cross_ref, out_ref):
    block = out_ref.shape[0]
    half = near_ref.shape[0] * near_ref.shape[2]
    q = q_ref[:, 0].reshape(block, HD)
    scores = [
        lax.dot_general(q, ref[:, 0].reshape(half, HD), NT, preferred_element_type=jnp.float32)
        for ref in (near_ref, far_ref)
    ]
    top = jnp.maximum(*[jnp.max(s, axis=1, keepdims=True) for s in scores])
    total = 0.0
    out = 0.0
    for s, ref in zip(scores, (near_ref, far_ref)):
        expo = jnp.exp2((s - top) * (SCALE * LOG2E))
        total += jnp.sum(expo, axis=1, keepdims=True)
        out += jnp.dot(
            expo.astype(jnp.bfloat16), ref[:, 1].reshape(half, HD), preferred_element_type=jnp.float32
        )
    out_ref[...] = (out / total + cross_ref[...]).astype(out_ref.dtype)


def self_attend(q_cot, near, far, cross_out, blocks=8):
    sources, _, rows, _ = q_cot.shape
    queries = sources * rows
    whole = pl.BlockSpec(near.shape, lambda j: (0, 0, 0, 0))
    return pl.pallas_call(
        self_kernel,
        grid=(blocks,),
        in_specs=[
            pl.BlockSpec((sources // blocks, 1, rows, HD), lambda j: (j, 0, 0, 0)),
            whole,
            whole,
            pl.BlockSpec((queries // blocks, HD), lambda j: (j, 0)),
        ],
        out_specs=pl.BlockSpec((queries // blocks, HD), lambda j: (j, 0)),
        out_shape=jax.ShapeDtypeStruct((queries, HD), jnp.bfloat16),
        compiler_params=pltpu.CompilerParams(vmem_limit_bytes=VMEM),
        cost_estimate=pl.CostEstimate(
            flops=8 * queries * queries * HD, bytes_accessed=5 * 1024 * 1024, transcendentals=2 * queries * queries
        ),
        name="self_attention",
    )(q_cot, near, far, cross_out)


def local(queries, keys, values, cotangent, captions, caption_len, proj_weight):
    side = lax.axis_index("g")
    core = lax.axis_index("c")
    n_ring = lax.axis_size("g") * lax.axis_size("d")
    n_dp = lax.axis_size("d")
    n_chips = lax.axis_size("y") * lax.axis_size("x")
    sides = lax.axis_size("g")
    side_arg = side.astype(jnp.int32).reshape(1)

    normed = normalize(captions[0])
    rows, features = normed.shape

    mine = lax.ppermute(
        proj_weight, PLANE, [(n_chips * c + i, sides * i + c) for c in range(sides) for i in range(n_chips)]
    )
    def place(z, c):
        g, d = divmod(z % n_ring, n_dp)
        return (g * sides + c) * n_dp + d

    def from_plane(distance, to):
        pairs = []
        for z in range(n_ring):
            g = z // n_dp
            pairs.append((place(z - distance, g), place(z, to)))
        return lax.ppermute(mine, ("g", "c", "d"), pairs)

    moved = lax.ppermute(
        mine, ("g", "c", "d"), [(place(z, z // n_dp), place(z, 1 - z // n_dp)) for z in range(n_ring)]
    )
    own = jnp.where(core == side, mine, moved)
    reach = n_dp // 2
    taken = []
    for t in range(1, reach + 1):
        block = from_plane(t, 0)
        if t < reach:
            block = jnp.where(core == 0, block, from_plane(-t, 1))
        taken.append(block)
    taken = jnp.stack(taken)
    other = lax.ppermute(taken, "c", SWAP)

    half_rows = lax.all_to_all(
        jnp.broadcast_to(normed[None], (n_chips, rows, features)), CHIPS, 0, 0, tiled=True
    ).reshape(n_chips * rows, features)
    spot = jnp.stack([lax.axis_index("d"), core]).astype(jnp.int32)
    text_half = project(spot, half_rows, own, taken, other)
    text_kv = lax.all_gather(text_half, "c", axis=0, tiled=True)

    q_cot = lax.all_to_all(pack(side_arg, queries, cotangent), PLANE, 0, 0, tiled=True)
    cross_out, kv_part = cross_attend(caption_len, q_cot, text_kv)

    half_tokens = kv_part.shape[0] // 2
    keep = lax.dynamic_slice_in_dim(kv_part, core * half_tokens, half_tokens, 0)
    give = lax.dynamic_slice_in_dim(kv_part, (1 - core) * half_tokens, half_tokens, 0)
    kv_half = (keep + lax.ppermute(give, "c", SWAP)).astype(jnp.bfloat16)
    kv_home = lax.ppermute(
        kv_half,
        ("g",) + PLANE,
        [
            (g * 2 * n_chips + 2 * i + c, c * 2 * n_chips + n_chips * g + i)
            for g in range(sides)
            for i in range(n_chips)
            for c in range(2)
        ],
    )
    kv_all = lax.all_gather(kv_home, RING, axis=0, tiled=True)

    blocks = normed.reshape(rows, n_dp, features // n_dp).transpose(1, 0, 2)
    by_sample = lax.all_to_all(blocks, "d", 0, 0, tiled=True)
    spread = lax.all_gather(by_sample, ("c",) + CHIPS, axis=0, tiled=False)
    spread = spread.reshape(2, n_chips, n_dp, rows, features // n_dp).transpose(0, 2, 1, 3, 4)
    spread = spread.reshape(2 * n_chips * n_dp * rows, features // n_dp)

    near = lax.all_to_all(pack(side_arg, keys, values), PLANE, 0, 0, tiled=True)
    far = lax.ppermute(near, "c", SWAP)
    out_rows = self_attend(q_cot, near, far, cross_out)
    back = lax.all_to_all(out_rows.reshape(near.shape[0], near.shape[2], HD), PLANE, 0, 0, tiled=True)
    attended = unpack(back)

    proj_grad = lax.dot_general(spread, kv_all, TN, preferred_element_type=jnp.float32)
    return attended, proj_grad


def solution(mesh):
    inner = Mesh(mesh.devices.reshape(2, 4, 4, 2, 8), ("g", "y", "x", "c", "d"))
    return jax.shard_map(
        local,
        mesh=inner,
        in_specs=(
            P("d", PLANE, None),
            P("d", PLANE, None),
            P("d", PLANE, "g"),
            P("d", PLANE, "g"),
            P("d", PLANE, None),
            P("d"),
            P("d", PLANE),
        ),
        out_specs=(P("d", PLANE, "g"), P("d", PLANE)),
        check_vma=False,
    )
```

```python
import math

import jax
import jax.numpy as jnp
from jax import lax
from jax.experimental import pallas as pl
from jax.experimental.pallas import tpu as pltpu
from jax.sharding import Mesh
from jax.sharding import PartitionSpec as P

HD = 128
SCALE = 1.0 / math.sqrt(HD)
LOG2E = math.log2(math.e)
PLANE = ("y", "x", "c")
RING = ("g", "d")
NT = (((1,), (1,)), ((), ()))
TN = (((0,), (0,)), ((), ()))
MIB = 1024 * 1024
SWAP = [(0, 1), (1, 0)]


def column_of(chip, chips, side):
    half = chips // 2
    return pl.multiple_of((2 * (chip % half) + lax.rem(chip // half + side, 2)) * HD, HD)


def prepare_kernel(
    spot_ref, wide_any, half_any, text_any, out_ref, blocks_ref, wide_ref, half_ref, text_ref, normed_ref, sems
):
    here = spot_ref[1]
    dests = out_ref.shape[0]
    width = half_any.shape[2]
    columns = pl.ds(pl.multiple_of(spot_ref[0] * width, width), width)
    copies = [
        pltpu.make_async_copy(text_any, text_ref, sems.at[0]),
        pltpu.make_async_copy(wide_any.at[:, :, columns], wide_ref, sems.at[1]),
        pltpu.make_async_copy(half_any, half_ref, sems.at[2]),
    ]
    for copy in copies:
        copy.start()
    copies[0].wait()
    n_dp, text_rows, depth = blocks_ref.shape
    rows = half_ref.shape[1] // 2
    wide = text_ref[0].astype(jnp.float32)
    square = jnp.mean(wide * wide, axis=-1, keepdims=True)
    normed_ref[...] = (wide * lax.rsqrt(square + 1e-06)).astype(jnp.bfloat16)
    for block in range(n_dp):
        blocks_ref[block] = normed_ref[:, block * depth : (block + 1) * depth]
    copies[1].wait()
    copies[2].wait()
    slots = n_dp // 2
    start = slots * depth // HD * text_rows
    for part in range(2):
        for slot in range(slots):
            away = (slot or slots) if part else -slot
            block = lax.rem(here + away + n_dp, n_dp)
            for lane in range(depth // HD):
                column = pl.multiple_of(block * depth + lane * HD, HD)
                piece = normed_ref[:, pl.ds(column, HD)]
                place = (slot * (depth // HD) + lane) * text_rows
                for head in range(dests // 2):
                    out_ref[2 * head + part, place : place + text_rows] = piece
        for head in range(dests // 2):
            columns = pl.ds(column_of(head, dests // 2, spot_ref[0]), HD)
            for slot, ref in enumerate((wide_ref, half_ref)):
                out_ref[2 * head + part, start + slot * rows : start + (slot + 1) * rows] = ref[
                    0, part * rows : (part + 1) * rows, columns
                ]


def prepare(spot, wide, half, text, n_dp):
    _, rows, width = half.shape
    _, text_rows, features = text.shape
    dests = 2 * width // HD
    pieces = features // 2 // HD * text_rows + rows
    depth = features // n_dp
    return pl.pallas_call(
        prepare_kernel,
        grid_spec=pltpu.PrefetchScalarGridSpec(
            num_scalar_prefetch=1,
            grid=(1,),
            in_specs=[pl.BlockSpec(memory_space=pltpu.HBM)] * 3,
            out_specs=[
                pl.BlockSpec((dests, pieces, HD), lambda j, spot_ref: (0, 0, 0)),
                pl.BlockSpec((n_dp, text_rows, depth), lambda j, spot_ref: (0, 0, 0)),
            ],
            scratch_shapes=[
                pltpu.VMEM(half.shape, half.dtype),
                pltpu.VMEM(half.shape, half.dtype),
                pltpu.VMEM(text.shape, text.dtype),
                pltpu.VMEM((text_rows, features), jnp.bfloat16),
                pltpu.SemaphoreType.DMA((3,)),
            ],
        ),
        out_shape=[
            jax.ShapeDtypeStruct((dests, pieces, HD), half.dtype),
            jax.ShapeDtypeStruct((n_dp, text_rows, depth), half.dtype),
        ],
        compiler_params=pltpu.CompilerParams(vmem_limit_bytes=16 * MIB),
        cost_estimate=pl.CostEstimate(
            flops=4 * text.size, bytes_accessed=2 * dests * pieces * HD + 4 * rows * width, transcendentals=0
        ),
        name="prepare",
    )(spot, wide, half, text)


def pack_kernel(spot_ref, wide_ref, half_ref, out_ref):
    rows = out_ref.shape[2]
    for dest in range(out_ref.shape[0]):
        head, part = dest // 2, dest % 2
        columns = pl.ds(column_of(head, out_ref.shape[0] // 2, spot_ref[0]), HD)
        for slot, ref in enumerate((wide_ref, half_ref)):
            out_ref[dest, slot] = ref[0, part * rows : (part + 1) * rows, columns]


def pack(spot, wide, half):
    _, rows, width = half.shape
    dests = 2 * width // HD
    return pl.pallas_call(
        pack_kernel,
        grid_spec=pltpu.PrefetchScalarGridSpec(
            num_scalar_prefetch=1,
            grid=(1,),
            in_specs=[
                pl.BlockSpec((1, rows, width), lambda j, spot_ref: (0, 0, spot_ref[0])),
                pl.BlockSpec((1, rows, width), lambda j, spot_ref: (0, 0, 0)),
            ],
            out_specs=pl.BlockSpec((dests, 2, rows // 2, HD), lambda j, spot_ref: (0, 0, 0, 0)),
        ),
        out_shape=jax.ShapeDtypeStruct((dests, 2, rows // 2, HD), half.dtype),
        compiler_params=pltpu.CompilerParams(vmem_limit_bytes=12 * MIB),
        cost_estimate=pl.CostEstimate(flops=0, bytes_accessed=4 * rows * width * 2, transcendentals=0),
        name="pack",
    )(spot, wide, half)


def unpack_kernel(spot_ref, in_ref, out_ref):
    rows = in_ref.shape[1]
    for source in range(in_ref.shape[0]):
        head, part = source // 2, source % 2
        columns = pl.ds(column_of(head, in_ref.shape[0] // 2, spot_ref[0]), HD)
        out_ref[0, part * rows : (part + 1) * rows, columns] = in_ref[source]


def unpack(spot, pieces):
    sources, rows, _ = pieces.shape
    width = sources // 2 * HD
    return pl.pallas_call(
        unpack_kernel,
        in_specs=[pl.BlockSpec(memory_space=pltpu.SMEM), pl.BlockSpec(memory_space=pltpu.VMEM)],
        out_shape=jax.ShapeDtypeStruct((1, 2 * rows, width), pieces.dtype),
        compiler_params=pltpu.CompilerParams(vmem_limit_bytes=8 * MIB),
        cost_estimate=pl.CostEstimate(flops=0, bytes_accessed=8 * rows * width, transcendentals=0),
        name="unpack",
    )(spot, pieces)


def project_kernel(spot_ref, text_ref, *refs):
    weight_refs, (out_ref, full_ref, half_ref, sems) = refs[:6], refs[6:]
    depth = full_ref.shape[1]
    groups = depth // HD
    sources = text_ref.shape[0]
    rows = out_ref.shape[0] // sources
    slots = [full_ref.at[k] for k in range(4)] + [half_ref.at[k] for k in range(2)]
    copies = [
        pltpu.make_async_copy(source, slot, sems.at[k])
        for k, (source, slot) in enumerate(zip(weight_refs, slots))
    ]
    for copy in copies:
        copy.start()
    for copy in copies:
        copy.wait()
    far = jnp.concatenate([half_ref[0], half_ref[1]], axis=1)
    weights = [jnp.where(spot_ref[2] == 0, full_ref[0], far), full_ref[1], full_ref[2], full_ref[3]]
    total = 0.0
    for slot, weight in enumerate(weights):
        block = jnp.concatenate(
            [
                text_ref[:, (slot * groups + k) * rows : (slot * groups + k + 1) * rows].reshape(sources * rows, HD)
                for k in range(groups)
            ],
            axis=1,
        )
        total += jnp.dot(block, weight, preferred_element_type=jnp.float32)
    out_ref[...] = total


def project(spot, received, text_rows, weights):
    sources = received.shape[0]
    depth, columns = weights[0].shape
    pieces = 4 * depth // HD * text_rows
    return pl.pallas_call(
        project_kernel,
        grid=(1,),
        in_specs=[
            pl.BlockSpec(memory_space=pltpu.SMEM),
            pl.BlockSpec((sources, pieces, HD), lambda j: (0, 0, 0)),
            *[pl.BlockSpec(memory_space=pltpu.HBM)] * 6,
        ],
        out_specs=pl.BlockSpec((sources * text_rows, columns), lambda j: (0, 0)),
        out_shape=jax.ShapeDtypeStruct((sources * text_rows, columns), jnp.float32),
        scratch_shapes=[
            pltpu.VMEM((4, depth, columns), jnp.bfloat16),
            pltpu.VMEM((2, depth, columns // 2), jnp.bfloat16),
            pltpu.SemaphoreType.DMA((6,)),
        ],
        compiler_params=pltpu.CompilerParams(vmem_limit_bytes=16 * MIB),
        cost_estimate=pl.CostEstimate(
            flops=8 * sources * text_rows * depth * columns, bytes_accessed=4 * MIB, transcendentals=0
        ),
        name="project",
    )(spot, received, *weights)


def cross_kernel(length_ref, spot_ref, q_ref, c_ref, near_ref, far_ref, out_ref, keep_ref, give_ref, total_ref):
    step = pl.program_id(0)
    block = out_ref.shape[0]
    tokens = near_ref.shape[0]
    q = q_ref[...].reshape(block, HD)
    cot = c_ref[...].reshape(block, HD)
    text_kv = (near_ref[...] + far_ref[...]).astype(jnp.bfloat16)
    text_keys = text_kv[:, :HD]
    text_vals = text_kv[:, HD:]
    live = lax.broadcasted_iota(jnp.int32, (tokens, 1), 0) < length_ref[0]
    scores = lax.dot_general(text_keys, q, NT, preferred_element_type=jnp.float32) * SCALE
    scores = jnp.where(live, scores, -jnp.inf)
    top = jnp.max(scores, axis=0, keepdims=True)
    expo = jnp.exp(scores - top)
    soft = expo / jnp.sum(expo, axis=0, keepdims=True)
    soft_low = soft.astype(jnp.bfloat16)
    out_t = lax.dot_general(text_vals, soft_low, TN, preferred_element_type=jnp.float32)
    out_ref[...] = out_t.T
    back = lax.dot_general(text_vals, cot, NT, preferred_element_type=jnp.float32)
    inner = jnp.sum(soft * back, axis=0, keepdims=True)
    grad_scores = (soft * (back - inner) * SCALE).astype(jnp.bfloat16)
    grad_keys = jnp.dot(grad_scores, q, preferred_element_type=jnp.float32)
    grad_vals = jnp.dot(soft_low, cot, preferred_element_type=jnp.float32)

    grads = jnp.concatenate([grad_keys, grad_vals], axis=1).reshape(total_ref.shape)

    @pl.when(step == 0)
    def _():
        total_ref[...] = grads

    @pl.when(step > 0)
    def _():
        total_ref[...] += grads

    @pl.when(step == pl.num_programs(0) - 1)
    def _():
        core = spot_ref[2]
        keep_ref[...] = total_ref[:, core].reshape(keep_ref.shape)
        give_ref[...] = total_ref[:, 1 - core].reshape(give_ref.shape)


def cross_attend(length, spot, received, rows, near, far, blocks=4):
    sources, pieces, _ = received.shape
    queries = sources * rows
    tokens, columns = near.shape
    last = pieces // rows
    text = pl.BlockSpec((tokens, columns), lambda j, n, s: (0, 0))
    half = pl.BlockSpec((tokens // 2, columns), lambda j, n, s: (0, 0))
    return pl.pallas_call(
        cross_kernel,
        grid_spec=pltpu.PrefetchScalarGridSpec(
            num_scalar_prefetch=2,
            grid=(blocks,),
            in_specs=[
                pl.BlockSpec((sources // blocks, rows, HD), lambda j, n, s: (j, last - 2, 0)),
                pl.BlockSpec((sources // blocks, rows, HD), lambda j, n, s: (j, last - 1, 0)),
                text,
                text,
            ],
            out_specs=[pl.BlockSpec((queries // blocks, HD), lambda j, n, s: (j, 0)), half, half],
            scratch_shapes=[pltpu.VMEM((sources // 2, 2, tokens // sources, columns), jnp.float32)],
        ),
        out_shape=[
            jax.ShapeDtypeStruct((queries, HD), jnp.float32),
            jax.ShapeDtypeStruct((tokens // 2, columns), jnp.float32),
            jax.ShapeDtypeStruct((tokens // 2, columns), jnp.float32),
        ],
        compiler_params=pltpu.CompilerParams(vmem_limit_bytes=24 * MIB),
        cost_estimate=pl.CostEstimate(
            flops=10 * queries * tokens * HD, bytes_accessed=4 * MIB, transcendentals=queries * tokens
        ),
        name="cross",
    )(length, spot, received, received, near, far)


def self_kernel(q_ref, near_ref, far_ref, cross_ref, out_ref):
    block = out_ref.shape[0]
    half = near_ref.shape[0] * near_ref.shape[2]
    q = q_ref[...].reshape(block, HD)
    scores = [
        lax.dot_general(q, ref[:, 0].reshape(half, HD), NT, preferred_element_type=jnp.float32)
        for ref in (near_ref, far_ref)
    ]
    top = jnp.maximum(*[jnp.max(s, axis=1, keepdims=True) for s in scores])
    total = 0.0
    out = 0.0
    for s, ref in zip(scores, (near_ref, far_ref)):
        expo = jnp.exp2((s - top) * (SCALE * LOG2E))
        total += jnp.sum(expo, axis=1, keepdims=True)
        out += jnp.dot(
            expo.astype(jnp.bfloat16), ref[:, 1].reshape(half, HD), preferred_element_type=jnp.float32
        )
    out_ref[...] = (out / total + cross_ref[...]).astype(out_ref.dtype)


def self_attend(received, near, far, cross_out, blocks=8):
    sources, _, rows, _ = near.shape
    queries = sources * rows
    last = received.shape[1] // rows
    whole = pl.BlockSpec(near.shape, lambda j: (0, 0, 0, 0))
    return pl.pallas_call(
        self_kernel,
        grid=(blocks,),
        in_specs=[
            pl.BlockSpec((sources // blocks, rows, HD), lambda j: (j, last - 2, 0)),
            whole,
            whole,
            pl.BlockSpec((queries // blocks, HD), lambda j: (j, 0)),
        ],
        out_specs=pl.BlockSpec((queries // blocks, HD), lambda j: (j, 0)),
        out_shape=jax.ShapeDtypeStruct((queries, HD), jnp.bfloat16),
        compiler_params=pltpu.CompilerParams(vmem_limit_bytes=36 * MIB),
        cost_estimate=pl.CostEstimate(
            flops=8 * queries * queries * HD, bytes_accessed=5 * MIB, transcendentals=2 * queries * queries
        ),
        name="self_attention",
    )(received, near, far, cross_out)


def finish_kernel(spot_ref, text_ref, kv_ref, keep_ref, give_ref):
    core, home = spot_ref[2], spot_ref[3]
    n_dp = text_ref.shape[1]
    tokens = kv_ref.shape[1]
    wanted = lax.rem(home + core, 2)
    keep, give = 0.0, 0.0
    for sample in range(n_dp):
        text = text_ref[:, sample].reshape(tokens, text_ref.shape[3])
        keep += lax.dot_general(text, kv_ref[wanted * n_dp + sample], TN, preferred_element_type=jnp.float32)
        give += lax.dot_general(text, kv_ref[(1 - wanted) * n_dp + sample], TN, preferred_element_type=jnp.float32)
    keep_ref[...] = keep
    give_ref[...] = give


def finish(spot, text, kv_all):
    depth = text.shape[3]
    columns = kv_all.shape[2]
    vmem = pl.BlockSpec(memory_space=pltpu.VMEM)
    return pl.pallas_call(
        finish_kernel,
        in_specs=[pl.BlockSpec(memory_space=pltpu.SMEM), vmem, vmem],
        out_specs=[vmem, vmem],
        out_shape=[jax.ShapeDtypeStruct((depth, columns), jnp.float32)] * 2,
        compiler_params=pltpu.CompilerParams(vmem_limit_bytes=20 * MIB),
        cost_estimate=pl.CostEstimate(flops=4 * text.size * columns, bytes_accessed=6 * MIB, transcendentals=0),
        name="finish",
    )(spot, text, kv_all)


def local(queries, keys, values, cotangent, captions, caption_len, proj_weight):
    side, turn, core = lax.axis_index("g"), lax.axis_index("d"), lax.axis_index("c")
    sides, n_dp = lax.axis_size("g"), lax.axis_size("d")
    n_ring = sides * n_dp
    n_chips = lax.axis_size("y") * lax.axis_size("x")
    home_side = lax.axis_index("y") // (lax.axis_size("y") // 2)
    spot = jnp.stack([side, turn, core, home_side]).astype(jnp.int32)
    text_rows, features = captions.shape[1:]

    def across(chip):
        return (chip + n_chips // 2) % n_chips

    passed = lax.ppermute(
        proj_weight,
        PLANE,
        [(2 * j, 2 * j + 1) for j in range(n_chips)] + [(2 * j + 1, 2 * across(j)) for j in range(n_chips)],
    )
    second = lax.ppermute(proj_weight, PLANE, [(2 * j + 1, 2 * across(j) + 1) for j in range(n_chips)])
    sent, blocks = prepare(spot, queries, cotangent, captions, n_dp)

    sent, passed, second = lax.optimization_barrier((sent, passed, second))
    received = lax.all_to_all(sent, PLANE, 0, 0, tiled=True)
    at_home = jnp.where(core == 0, proj_weight, passed)
    away = jnp.where(core == 0, passed, second)
    head_of_side = (jnp.where(home_side == 0, at_home, away), jnp.where(home_side == 0, away, at_home))

    def place(z, c):
        g, d = divmod(z % n_ring, n_dp)
        return (g * sides + c) * n_dp + d

    def block_for(distance):
        to_side = (side * n_dp + turn + distance + n_ring) % n_ring // n_dp
        return jnp.where(to_side == 0, head_of_side[0], head_of_side[1])

    def send(block, up, down):
        pairs = [(place(z, 0), place(z + up, 0)) for z in range(n_ring) if up]
        pairs += [(place(z, 1), place(z + down, 1)) for z in range(n_ring)]
        return lax.ppermute(block, ("g", "c", "d"), pairs)

    reach = n_dp // 2
    weights = [jnp.where(side == 0, head_of_side[0], head_of_side[1])]
    weights += [send(block_for((1 - 2 * core) * t), t, -t) for t in range(1, reach)]
    weights.append(send(block_for(-reach)[:, :HD], 0, -reach))
    weights.append(send(block_for(reach)[:, HD:], 0, reach))

    received, keys, values = lax.optimization_barrier((received, keys, values))
    near = lax.all_to_all(pack(spot, keys, values), PLANE, 0, 0, tiled=True)

    text_near = project(spot, received, text_rows, weights)
    text_far = lax.ppermute(text_near, "c", SWAP)
    rows = queries.shape[1] // 2
    cross_out, keep, give = cross_attend(caption_len, spot, received, rows, text_near, text_far)

    kv_half = (keep + lax.ppermute(give, "c", SWAP)).astype(jnp.bfloat16)
    kv_half, near, blocks = lax.optimization_barrier((kv_half, near, blocks))

    kv_all = lax.all_gather(kv_half, RING, axis=0, tiled=False)

    by_sample = lax.all_to_all(blocks, "d", 0, 0, tiled=True)
    spread = lax.all_to_all(
        jnp.broadcast_to(by_sample[None], (n_chips,) + by_sample.shape), ("y", "x"), 0, 0, tiled=True
    )

    far = lax.ppermute(near, "c", SWAP)
    out_rows = self_attend(received, near, far, cross_out)
    back = lax.all_to_all(out_rows.reshape(near.shape[0], rows, HD), PLANE, 0, 0, tiled=True)
    attended = unpack(spot, back)

    spread, back = lax.optimization_barrier((spread, back))
    keep, give = finish(spot, spread, kv_all)
    total = keep + lax.ppermute(give, "c", SWAP)
    moved = lax.ppermute(total, PLANE, [(2 * j + 1, 2 * across(j) + 1) for j in range(n_chips)])
    proj_grad = jnp.where(core == 0, total, moved)
    return attended, proj_grad


def solution(mesh):
    inner = Mesh(mesh.devices.reshape(2, 4, 4, 2, 8), ("g", "y", "x", "c", "d"))
    return jax.shard_map(
        local,
        mesh=inner,
        in_specs=(
            P("d", PLANE, None),
            P("d", PLANE, None),
            P("d", PLANE, "g"),
            P("d", PLANE, "g"),
            P("d", PLANE, None),
            P("d"),
            P("d", PLANE),
        ),
        out_specs=(P("d", PLANE, "g"), P("d", PLANE)),
        check_vma=False,
    )
```

```python
import math

import jax
import jax.numpy as jnp
from jax import lax
from jax.experimental import pallas as pl
from jax.experimental.pallas import tpu as pltpu
from jax.sharding import Mesh
from jax.sharding import PartitionSpec as P

HD = 128
SCALE = 1.0 / math.sqrt(HD)
LOG2E = math.log2(math.e)
PLANE = ("y", "x", "c")
RING = ("g", "d")
NT = (((1,), (1,)), ((), ()))
TN = (((0,), (0,)), ((), ()))
MIB = 1024 * 1024
SWAP = [(0, 1), (1, 0)]


def column_of(chip, chips, side):
    half = chips // 2
    return pl.multiple_of((2 * (chip % half) + lax.rem(chip // half + side, 2)) * HD, HD)


def prepare_kernel(
    spot_ref, wide_any, half_any, text_any, out_ref, blocks_ref, wide_ref, half_ref, text_ref, normed_ref, sems
):
    here = spot_ref[1]
    dests = out_ref.shape[0]
    width = half_any.shape[2]
    columns = pl.ds(pl.multiple_of(spot_ref[0] * width, width), width)
    copies = [
        pltpu.make_async_copy(text_any, text_ref, sems.at[0]),
        pltpu.make_async_copy(wide_any.at[:, :, columns], wide_ref, sems.at[1]),
        pltpu.make_async_copy(half_any, half_ref, sems.at[2]),
    ]
    for copy in copies:
        copy.start()
    copies[0].wait()
    n_dp, text_rows, depth = blocks_ref.shape
    rows = half_ref.shape[1] // 2
    wide = text_ref[0].astype(jnp.float32)
    square = jnp.mean(wide * wide, axis=-1, keepdims=True)
    normed_ref[...] = (wide * lax.rsqrt(square + 1e-06)).astype(jnp.bfloat16)
    for block in range(n_dp):
        blocks_ref[block] = normed_ref[:, block * depth : (block + 1) * depth]
    copies[1].wait()
    copies[2].wait()
    slots = n_dp // 2
    start = slots * depth // HD * text_rows
    for part in range(2):
        for slot in range(slots):
            away = (slot or slots) if part else -slot
            block = lax.rem(here + away + n_dp, n_dp)
            for lane in range(depth // HD):
                column = pl.multiple_of(block * depth + lane * HD, HD)
                piece = normed_ref[:, pl.ds(column, HD)]
                place = (slot * (depth // HD) + lane) * text_rows
                for head in range(dests // 2):
                    out_ref[2 * head + part, place : place + text_rows] = piece
        for head in range(dests // 2):
            columns = pl.ds(column_of(head, dests // 2, spot_ref[0]), HD)
            for slot, ref in enumerate((wide_ref, half_ref)):
                out_ref[2 * head + part, start + slot * rows : start + (slot + 1) * rows] = ref[
                    0, part * rows : (part + 1) * rows, columns
                ]


def prepare(spot, wide, half, text, n_dp):
    _, rows, width = half.shape
    _, text_rows, features = text.shape
    dests = 2 * width // HD
    pieces = features // 2 // HD * text_rows + rows
    depth = features // n_dp
    return pl.pallas_call(
        prepare_kernel,
        grid_spec=pltpu.PrefetchScalarGridSpec(
            num_scalar_prefetch=1,
            grid=(1,),
            in_specs=[pl.BlockSpec(memory_space=pltpu.HBM)] * 3,
            out_specs=[
                pl.BlockSpec((dests, pieces, HD), lambda j, spot_ref: (0, 0, 0)),
                pl.BlockSpec((n_dp, text_rows, depth), lambda j, spot_ref: (0, 0, 0)),
            ],
            scratch_shapes=[
                pltpu.VMEM(half.shape, half.dtype),
                pltpu.VMEM(half.shape, half.dtype),
                pltpu.VMEM(text.shape, text.dtype),
                pltpu.VMEM((text_rows, features), jnp.bfloat16),
                pltpu.SemaphoreType.DMA((3,)),
            ],
        ),
        out_shape=[
            jax.ShapeDtypeStruct((dests, pieces, HD), half.dtype),
            jax.ShapeDtypeStruct((n_dp, text_rows, depth), half.dtype),
        ],
        compiler_params=pltpu.CompilerParams(vmem_limit_bytes=12 * MIB),
        cost_estimate=pl.CostEstimate(
            flops=4 * text.size, bytes_accessed=2 * dests * pieces * HD + 4 * rows * width, transcendentals=0
        ),
        name="prepare",
    )(spot, wide, half, text)


def pack_kernel(spot_ref, wide_ref, half_ref, out_ref):
    rows = out_ref.shape[2]
    for dest in range(out_ref.shape[0]):
        head, part = dest // 2, dest % 2
        columns = pl.ds(column_of(head, out_ref.shape[0] // 2, spot_ref[0]), HD)
        for slot, ref in enumerate((wide_ref, half_ref)):
            out_ref[dest, slot] = ref[0, part * rows : (part + 1) * rows, columns]


def pack(spot, wide, half):
    _, rows, width = half.shape
    dests = 2 * width // HD
    return pl.pallas_call(
        pack_kernel,
        grid_spec=pltpu.PrefetchScalarGridSpec(
            num_scalar_prefetch=1,
            grid=(1,),
            in_specs=[
                pl.BlockSpec((1, rows, width), lambda j, spot_ref: (0, 0, spot_ref[0])),
                pl.BlockSpec((1, rows, width), lambda j, spot_ref: (0, 0, 0)),
            ],
            out_specs=pl.BlockSpec((dests, 2, rows // 2, HD), lambda j, spot_ref: (0, 0, 0, 0)),
        ),
        out_shape=jax.ShapeDtypeStruct((dests, 2, rows // 2, HD), half.dtype),
        compiler_params=pltpu.CompilerParams(vmem_limit_bytes=8 * MIB),
        cost_estimate=pl.CostEstimate(flops=0, bytes_accessed=4 * rows * width * 2, transcendentals=0),
        name="pack",
    )(spot, wide, half)


def unpack_kernel(spot_ref, in_ref, out_ref):
    rows = in_ref.shape[1]
    for source in range(in_ref.shape[0]):
        head, part = source // 2, source % 2
        columns = pl.ds(column_of(head, in_ref.shape[0] // 2, spot_ref[0]), HD)
        out_ref[0, part * rows : (part + 1) * rows, columns] = in_ref[source]


def unpack(spot, pieces):
    sources, rows, _ = pieces.shape
    width = sources // 2 * HD
    return pl.pallas_call(
        unpack_kernel,
        in_specs=[pl.BlockSpec(memory_space=pltpu.SMEM), pl.BlockSpec(memory_space=pltpu.VMEM)],
        out_shape=jax.ShapeDtypeStruct((1, 2 * rows, width), pieces.dtype),
        compiler_params=pltpu.CompilerParams(vmem_limit_bytes=4 * MIB),
        cost_estimate=pl.CostEstimate(flops=0, bytes_accessed=8 * rows * width, transcendentals=0),
        name="unpack",
    )(spot, pieces)


def project_kernel(spot_ref, text_ref, *refs):
    weight_refs, (out_ref, full_ref, half_ref, sems) = refs[:6], refs[6:]
    depth = full_ref.shape[1]
    groups = depth // HD
    sources = text_ref.shape[0]
    rows = out_ref.shape[0] // sources
    slots = [full_ref.at[k] for k in range(4)] + [half_ref.at[k] for k in range(2)]
    copies = [
        pltpu.make_async_copy(source, slot, sems.at[k])
        for k, (source, slot) in enumerate(zip(weight_refs, slots))
    ]
    for copy in copies:
        copy.start()
    for copy in copies:
        copy.wait()
    far = jnp.concatenate([half_ref[0], half_ref[1]], axis=1)
    weights = [jnp.where(spot_ref[2] == 0, full_ref[0], far), full_ref[1], full_ref[2], full_ref[3]]
    total = 0.0
    for slot, weight in enumerate(weights):
        block = jnp.concatenate(
            [
                text_ref[:, (slot * groups + k) * rows : (slot * groups + k + 1) * rows].reshape(sources * rows, HD)
                for k in range(groups)
            ],
            axis=1,
        )
        total += jnp.dot(block, weight, preferred_element_type=jnp.float32)
    out_ref[...] = total


def project(spot, received, text_rows, weights):
    sources = received.shape[0]
    depth, columns = weights[0].shape
    pieces = 4 * depth // HD * text_rows
    return pl.pallas_call(
        project_kernel,
        grid=(1,),
        in_specs=[
            pl.BlockSpec(memory_space=pltpu.SMEM),
            pl.BlockSpec((sources, pieces, HD), lambda j: (0, 0, 0)),
            *[pl.BlockSpec(memory_space=pltpu.HBM)] * 6,
        ],
        out_specs=pl.BlockSpec((sources * text_rows, columns), lambda j: (0, 0)),
        out_shape=jax.ShapeDtypeStruct((sources * text_rows, columns), jnp.float32),
        scratch_shapes=[
            pltpu.VMEM((4, depth, columns), jnp.bfloat16),
            pltpu.VMEM((2, depth, columns // 2), jnp.bfloat16),
            pltpu.SemaphoreType.DMA((6,)),
        ],
        compiler_params=pltpu.CompilerParams(vmem_limit_bytes=10 * MIB),
        cost_estimate=pl.CostEstimate(
            flops=8 * sources * text_rows * depth * columns, bytes_accessed=4 * MIB, transcendentals=0
        ),
        name="project",
    )(spot, received, *weights)


def cross_kernel(length_ref, spot_ref, q_ref, c_ref, near_ref, far_ref, out_ref, keep_ref, give_ref, total_ref):
    step = pl.program_id(0)
    block = out_ref.shape[0]
    tokens = near_ref.shape[0]
    q = q_ref[...].reshape(block, HD)
    cot = c_ref[...].reshape(block, HD)
    text_kv = (near_ref[...] + far_ref[...]).astype(jnp.bfloat16)
    text_keys = text_kv[:, :HD]
    text_vals = text_kv[:, HD:]
    live = lax.broadcasted_iota(jnp.int32, (tokens, 1), 0) < length_ref[0]
    scores = lax.dot_general(text_keys, q, NT, preferred_element_type=jnp.float32) * SCALE
    scores = jnp.where(live, scores, -jnp.inf)
    top = jnp.max(scores, axis=0, keepdims=True)
    expo = jnp.exp(scores - top)
    soft = expo / jnp.sum(expo, axis=0, keepdims=True)
    soft_low = soft.astype(jnp.bfloat16)
    out_t = lax.dot_general(text_vals, soft_low, TN, preferred_element_type=jnp.float32)
    out_ref[...] = out_t.T
    back = lax.dot_general(text_vals, cot, NT, preferred_element_type=jnp.float32)
    inner = jnp.sum(soft * back, axis=0, keepdims=True)
    grad_scores = (soft * (back - inner) * SCALE).astype(jnp.bfloat16)
    grad_keys = jnp.dot(grad_scores, q, preferred_element_type=jnp.float32)
    grad_vals = jnp.dot(soft_low, cot, preferred_element_type=jnp.float32)

    grads = jnp.concatenate([grad_keys, grad_vals], axis=1).reshape(total_ref.shape)

    @pl.when(step == 0)
    def _():
        total_ref[...] = grads

    @pl.when(step > 0)
    def _():
        total_ref[...] += grads

    @pl.when(step == pl.num_programs(0) - 1)
    def _():
        core = spot_ref[2]
        keep_ref[...] = total_ref[:, core].reshape(keep_ref.shape)
        give_ref[...] = total_ref[:, 1 - core].reshape(give_ref.shape)


def cross_attend(length, spot, received, rows, near, far, blocks=2):
    sources, pieces, _ = received.shape
    queries = sources * rows
    tokens, columns = near.shape
    last = pieces // rows
    text = pl.BlockSpec((tokens, columns), lambda j, n, s: (0, 0))
    half = pl.BlockSpec((tokens // 2, columns), lambda j, n, s: (0, 0))
    return pl.pallas_call(
        cross_kernel,
        grid_spec=pltpu.PrefetchScalarGridSpec(
            num_scalar_prefetch=2,
            grid=(blocks,),
            in_specs=[
                pl.BlockSpec((sources // blocks, rows, HD), lambda j, n, s: (j, last - 2, 0)),
                pl.BlockSpec((sources // blocks, rows, HD), lambda j, n, s: (j, last - 1, 0)),
                text,
                text,
            ],
            out_specs=[pl.BlockSpec((queries // blocks, HD), lambda j, n, s: (j, 0)), half, half],
            scratch_shapes=[pltpu.VMEM((sources // 2, 2, tokens // sources, columns), jnp.float32)],
        ),
        out_shape=[
            jax.ShapeDtypeStruct((queries, HD), jnp.float32),
            jax.ShapeDtypeStruct((tokens // 2, columns), jnp.float32),
            jax.ShapeDtypeStruct((tokens // 2, columns), jnp.float32),
        ],
        compiler_params=pltpu.CompilerParams(vmem_limit_bytes=20 * MIB),
        cost_estimate=pl.CostEstimate(
            flops=10 * queries * tokens * HD, bytes_accessed=4 * MIB, transcendentals=queries * tokens
        ),
        name="cross",
    )(length, spot, received, received, near, far)


def self_kernel(q_ref, near_ref, far_ref, cross_ref, out_ref):
    block = out_ref.shape[0]
    half = near_ref.shape[0] * near_ref.shape[2]
    q = q_ref[...].reshape(block, HD)
    scores = [
        lax.dot_general(q, ref[:, 0].reshape(half, HD), NT, preferred_element_type=jnp.float32)
        for ref in (near_ref, far_ref)
    ]
    top = jnp.maximum(*[jnp.max(s, axis=1, keepdims=True) for s in scores])
    total = 0.0
    out = 0.0
    for s, ref in zip(scores, (near_ref, far_ref)):
        expo = jnp.exp2((s - top) * (SCALE * LOG2E))
        total += jnp.sum(expo, axis=1, keepdims=True)
        out += jnp.dot(
            expo.astype(jnp.bfloat16), ref[:, 1].reshape(half, HD), preferred_element_type=jnp.float32
        )
    out_ref[...] = (out / total + cross_ref[...]).astype(out_ref.dtype)


def self_attend(received, near, far, cross_out, blocks=8):
    sources, _, rows, _ = near.shape
    queries = sources * rows
    last = received.shape[1] // rows
    whole = pl.BlockSpec(near.shape, lambda j: (0, 0, 0, 0))
    return pl.pallas_call(
        self_kernel,
        grid=(blocks,),
        in_specs=[
            pl.BlockSpec((sources // blocks, rows, HD), lambda j: (j, last - 2, 0)),
            whole,
            whole,
            pl.BlockSpec((queries // blocks, HD), lambda j: (j, 0)),
        ],
        out_specs=pl.BlockSpec((queries // blocks, HD), lambda j: (j, 0)),
        out_shape=jax.ShapeDtypeStruct((queries, HD), jnp.bfloat16),
        compiler_params=pltpu.CompilerParams(vmem_limit_bytes=20 * MIB),
        cost_estimate=pl.CostEstimate(
            flops=8 * queries * queries * HD, bytes_accessed=5 * MIB, transcendentals=2 * queries * queries
        ),
        name="self_attention",
    )(received, near, far, cross_out)


def finish_kernel(spot_ref, text_ref, kv_ref, keep_ref, give_ref):
    core, home = spot_ref[2], spot_ref[3]
    n_dp = text_ref.shape[1]
    tokens = kv_ref.shape[1]
    wanted = lax.rem(home + core, 2)
    keep, give = 0.0, 0.0
    for sample in range(n_dp):
        text = text_ref[:, sample].reshape(tokens, text_ref.shape[3])
        keep += lax.dot_general(text, kv_ref[wanted * n_dp + sample], TN, preferred_element_type=jnp.float32)
        give += lax.dot_general(text, kv_ref[(1 - wanted) * n_dp + sample], TN, preferred_element_type=jnp.float32)
    keep_ref[...] = keep
    give_ref[...] = give


def finish(spot, text, kv_all):
    depth = text.shape[3]
    columns = kv_all.shape[2]
    vmem = pl.BlockSpec(memory_space=pltpu.VMEM)
    return pl.pallas_call(
        finish_kernel,
        in_specs=[pl.BlockSpec(memory_space=pltpu.SMEM), vmem, vmem],
        out_specs=[vmem, vmem],
        out_shape=[jax.ShapeDtypeStruct((depth, columns), jnp.float32)] * 2,
        compiler_params=pltpu.CompilerParams(vmem_limit_bytes=14 * MIB),
        cost_estimate=pl.CostEstimate(flops=4 * text.size * columns, bytes_accessed=6 * MIB, transcendentals=0),
        name="finish",
    )(spot, text, kv_all)


def local(queries, keys, values, cotangent, captions, caption_len, proj_weight):
    side, turn, core = lax.axis_index("g"), lax.axis_index("d"), lax.axis_index("c")
    sides, n_dp = lax.axis_size("g"), lax.axis_size("d")
    n_ring = sides * n_dp
    n_chips = lax.axis_size("y") * lax.axis_size("x")
    home_side = lax.axis_index("y") // (lax.axis_size("y") // 2)
    spot = jnp.stack([side, turn, core, home_side]).astype(jnp.int32)
    text_rows, features = captions.shape[1:]

    def across(chip):
        return (chip + n_chips // 2) % n_chips

    passed = lax.ppermute(
        proj_weight,
        PLANE,
        [(2 * j, 2 * j + 1) for j in range(n_chips)] + [(2 * j + 1, 2 * across(j)) for j in range(n_chips)],
    )
    second = lax.ppermute(proj_weight, PLANE, [(2 * j + 1, 2 * across(j) + 1) for j in range(n_chips)])
    sent, blocks = prepare(spot, queries, cotangent, captions, n_dp)

    sent, passed, second = lax.optimization_barrier((sent, passed, second))
    received = lax.all_to_all(sent, PLANE, 0, 0, tiled=True)
    at_home = jnp.where(core == 0, proj_weight, passed)
    away = jnp.where(core == 0, passed, second)
    head_of_side = (jnp.where(home_side == 0, at_home, away), jnp.where(home_side == 0, away, at_home))

    def place(z, c):
        g, d = divmod(z % n_ring, n_dp)
        return (g * sides + c) * n_dp + d

    def block_for(distance):
        to_side = (side * n_dp + turn + distance + n_ring) % n_ring // n_dp
        return jnp.where(to_side == 0, head_of_side[0], head_of_side[1])

    def send(block, up, down):
        pairs = [(place(z, 0), place(z + up, 0)) for z in range(n_ring) if up]
        pairs += [(place(z, 1), place(z + down, 1)) for z in range(n_ring)]
        return lax.ppermute(block, ("g", "c", "d"), pairs)

    reach = n_dp // 2
    weights = [jnp.where(side == 0, head_of_side[0], head_of_side[1])]
    weights += [send(block_for((1 - 2 * core) * t), t, -t) for t in range(1, reach)]
    weights.append(send(block_for(-reach)[:, :HD], 0, -reach))
    weights.append(send(block_for(reach)[:, HD:], 0, reach))

    received, keys, values = lax.optimization_barrier((received, keys, values))
    near = lax.all_to_all(pack(spot, keys, values), PLANE, 0, 0, tiled=True)

    text_near = project(spot, received, text_rows, weights)
    text_far = lax.ppermute(text_near, "c", SWAP)
    rows = queries.shape[1] // 2
    cross_out, keep, give = cross_attend(caption_len, spot, received, rows, text_near, text_far)

    kv_half = (keep + lax.ppermute(give, "c", SWAP)).astype(jnp.bfloat16)
    kv_half, near, blocks = lax.optimization_barrier((kv_half, near, blocks))

    kv_all = lax.all_gather(kv_half, RING, axis=0, tiled=False)

    by_sample = lax.all_to_all(blocks, "d", 0, 0, tiled=True)
    spread = lax.all_to_all(
        jnp.broadcast_to(by_sample[None], (n_chips,) + by_sample.shape), ("y", "x"), 0, 0, tiled=True
    )

    far = lax.ppermute(near, "c", SWAP)
    out_rows = self_attend(received, near, far, cross_out)
    spread, out_rows = lax.optimization_barrier((spread, out_rows))
    back = lax.all_to_all(out_rows.reshape(near.shape[0], rows, HD), PLANE, 0, 0, tiled=True)
    attended = unpack(spot, back)

    spread, back = lax.optimization_barrier((spread, back))
    keep, give = finish(spot, spread, kv_all)
    total = keep + lax.ppermute(give, "c", SWAP)
    moved = lax.ppermute(total, PLANE, [(2 * j + 1, 2 * across(j) + 1) for j in range(n_chips)])
    proj_grad = jnp.where(core == 0, total, moved)
    return attended, proj_grad


def solution(mesh):
    inner = Mesh(mesh.devices.reshape(2, 4, 4, 2, 8), ("g", "y", "x", "c", "d"))
    return jax.shard_map(
        local,
        mesh=inner,
        in_specs=(
            P("d", PLANE, None),
            P("d", PLANE, None),
            P("d", PLANE, "g"),
            P("d", PLANE, "g"),
            P("d", PLANE, None),
            P("d"),
            P("d", PLANE),
        ),
        out_specs=(P("d", PLANE, "g"), P("d", PLANE)),
        check_vma=False,
    )
```

```python
import math

import jax
import jax.numpy as jnp
from jax import lax
from jax.experimental import pallas as pl
from jax.experimental.pallas import tpu as pltpu
from jax.sharding import Mesh
from jax.sharding import PartitionSpec as P

HD = 128
SCALE = 1.0 / math.sqrt(HD)
LOG2E = math.log2(math.e)
PLANE = ("y", "x", "c")
RING = ("g", "d")
NT = (((1,), (1,)), ((), ()))
TN = (((0,), (0,)), ((), ()))
MIB = 1024 * 1024
SWAP = [(0, 1), (1, 0)]


def column_of(chip, chips, side):
    half = chips // 2
    return pl.multiple_of((2 * (chip % half) + lax.rem(chip // half + side, 2)) * HD, HD)


def prepare_kernel(
    spot_ref, wide_any, half_any, text_any, out_ref, blocks_ref, wide_ref, half_ref, text_ref, normed_ref, sems
):
    here = spot_ref[1]
    dests = out_ref.shape[0]
    width = half_any.shape[2]
    columns = pl.ds(pl.multiple_of(spot_ref[0] * width, width), width)
    copies = [
        pltpu.make_async_copy(text_any, text_ref, sems.at[0]),
        pltpu.make_async_copy(wide_any.at[:, :, columns], wide_ref, sems.at[1]),
        pltpu.make_async_copy(half_any, half_ref, sems.at[2]),
    ]
    for copy in copies:
        copy.start()
    copies[0].wait()
    n_dp, text_rows, depth = blocks_ref.shape
    rows = half_ref.shape[1] // 2
    wide = text_ref[0].astype(jnp.float32)
    square = jnp.mean(wide * wide, axis=-1, keepdims=True)
    normed_ref[...] = (wide * lax.rsqrt(square + 1e-06)).astype(jnp.bfloat16)
    for block in range(n_dp):
        blocks_ref[block] = normed_ref[:, block * depth : (block + 1) * depth]
    copies[1].wait()
    copies[2].wait()
    slots = n_dp // 2
    start = slots * depth // HD * text_rows
    for part in range(2):
        for slot in range(slots):
            away = (slot or slots) if part else -slot
            block = lax.rem(here + away + n_dp, n_dp)
            for lane in range(depth // HD):
                column = pl.multiple_of(block * depth + lane * HD, HD)
                piece = normed_ref[:, pl.ds(column, HD)]
                place = (slot * (depth // HD) + lane) * text_rows
                for head in range(dests // 2):
                    out_ref[2 * head + part, place : place + text_rows] = piece
        for head in range(dests // 2):
            columns = pl.ds(column_of(head, dests // 2, spot_ref[0]), HD)
            for slot, ref in enumerate((wide_ref, half_ref)):
                out_ref[2 * head + part, start + slot * rows : start + (slot + 1) * rows] = ref[
                    0, part * rows : (part + 1) * rows, columns
                ]


def prepare(spot, wide, half, text, n_dp):
    _, rows, width = half.shape
    _, text_rows, features = text.shape
    dests = 2 * width // HD
    pieces = features // 2 // HD * text_rows + rows
    depth = features // n_dp
    return pl.pallas_call(
        prepare_kernel,
        grid_spec=pltpu.PrefetchScalarGridSpec(
            num_scalar_prefetch=1,
            grid=(1,),
            in_specs=[pl.BlockSpec(memory_space=pltpu.HBM)] * 3,
            out_specs=[
                pl.BlockSpec((dests, pieces, HD), lambda j, spot_ref: (0, 0, 0)),
                pl.BlockSpec((n_dp, text_rows, depth), lambda j, spot_ref: (0, 0, 0)),
            ],
            scratch_shapes=[
                pltpu.VMEM(half.shape, half.dtype),
                pltpu.VMEM(half.shape, half.dtype),
                pltpu.VMEM(text.shape, text.dtype),
                pltpu.VMEM((text_rows, features), jnp.bfloat16),
                pltpu.SemaphoreType.DMA((3,)),
            ],
        ),
        out_shape=[
            jax.ShapeDtypeStruct((dests, pieces, HD), half.dtype),
            jax.ShapeDtypeStruct((n_dp, text_rows, depth), half.dtype),
        ],
        compiler_params=pltpu.CompilerParams(vmem_limit_bytes=12 * MIB),
        cost_estimate=pl.CostEstimate(
            flops=4 * text.size, bytes_accessed=2 * dests * pieces * HD + 4 * rows * width, transcendentals=0
        ),
        name="prepare",
    )(spot, wide, half, text)


def pack_kernel(spot_ref, wide_ref, half_ref, out_ref):
    rows = out_ref.shape[2]
    for dest in range(out_ref.shape[0]):
        head, part = dest // 2, dest % 2
        columns = pl.ds(column_of(head, out_ref.shape[0] // 2, spot_ref[0]), HD)
        for slot, ref in enumerate((wide_ref, half_ref)):
            out_ref[dest, slot] = ref[0, part * rows : (part + 1) * rows, columns]


def pack(spot, wide, half):
    _, rows, width = half.shape
    dests = 2 * width // HD
    return pl.pallas_call(
        pack_kernel,
        grid_spec=pltpu.PrefetchScalarGridSpec(
            num_scalar_prefetch=1,
            grid=(1,),
            in_specs=[
                pl.BlockSpec((1, rows, width), lambda j, spot_ref: (0, 0, spot_ref[0])),
                pl.BlockSpec((1, rows, width), lambda j, spot_ref: (0, 0, 0)),
            ],
            out_specs=pl.BlockSpec((dests, 2, rows // 2, HD), lambda j, spot_ref: (0, 0, 0, 0)),
        ),
        out_shape=jax.ShapeDtypeStruct((dests, 2, rows // 2, HD), half.dtype),
        compiler_params=pltpu.CompilerParams(vmem_limit_bytes=8 * MIB),
        cost_estimate=pl.CostEstimate(flops=0, bytes_accessed=4 * rows * width * 2, transcendentals=0),
        name="pack",
    )(spot, wide, half)


def unpack_kernel(spot_ref, in_ref, out_ref):
    rows = in_ref.shape[1]
    for source in range(in_ref.shape[0]):
        head, part = source // 2, source % 2
        columns = pl.ds(column_of(head, in_ref.shape[0] // 2, spot_ref[0]), HD)
        out_ref[0, part * rows : (part + 1) * rows, columns] = in_ref[source]


def unpack(spot, pieces):
    sources, rows, _ = pieces.shape
    width = sources // 2 * HD
    return pl.pallas_call(
        unpack_kernel,
        in_specs=[pl.BlockSpec(memory_space=pltpu.SMEM), pl.BlockSpec(memory_space=pltpu.VMEM)],
        out_shape=jax.ShapeDtypeStruct((1, 2 * rows, width), pieces.dtype),
        compiler_params=pltpu.CompilerParams(vmem_limit_bytes=4 * MIB),
        cost_estimate=pl.CostEstimate(flops=0, bytes_accessed=8 * rows * width, transcendentals=0),
        name="unpack",
    )(spot, pieces)


def project_kernel(spot_ref, text_ref, *refs):
    weight_refs, (out_ref, full_ref, half_ref, sems) = refs[:6], refs[6:]
    depth = full_ref.shape[1]
    groups = depth // HD
    sources = text_ref.shape[0]
    rows = out_ref.shape[0] // sources
    slots = [full_ref.at[k] for k in range(4)] + [half_ref.at[k] for k in range(2)]
    copies = [
        pltpu.make_async_copy(source, slot, sems.at[k])
        for k, (source, slot) in enumerate(zip(weight_refs, slots))
    ]
    for copy in copies:
        copy.start()
    for copy in copies:
        copy.wait()
    far = jnp.concatenate([half_ref[0], half_ref[1]], axis=1)
    weights = [jnp.where(spot_ref[2] == 0, full_ref[0], far), full_ref[1], full_ref[2], full_ref[3]]
    total = 0.0
    for slot, weight in enumerate(weights):
        block = jnp.concatenate(
            [
                text_ref[:, (slot * groups + k) * rows : (slot * groups + k + 1) * rows].reshape(sources * rows, HD)
                for k in range(groups)
            ],
            axis=1,
        )
        total += jnp.dot(block, weight, preferred_element_type=jnp.float32)
    out_ref[...] = total


def project(spot, received, text_rows, weights):
    sources = received.shape[0]
    depth, columns = weights[0].shape
    pieces = 4 * depth // HD * text_rows
    return pl.pallas_call(
        project_kernel,
        grid=(1,),
        in_specs=[
            pl.BlockSpec(memory_space=pltpu.SMEM),
            pl.BlockSpec((sources, pieces, HD), lambda j: (0, 0, 0)),
            *[pl.BlockSpec(memory_space=pltpu.HBM)] * 6,
        ],
        out_specs=pl.BlockSpec((sources * text_rows, columns), lambda j: (0, 0)),
        out_shape=jax.ShapeDtypeStruct((sources * text_rows, columns), jnp.float32),
        scratch_shapes=[
            pltpu.VMEM((4, depth, columns), jnp.bfloat16),
            pltpu.VMEM((2, depth, columns // 2), jnp.bfloat16),
            pltpu.SemaphoreType.DMA((6,)),
        ],
        compiler_params=pltpu.CompilerParams(vmem_limit_bytes=10 * MIB),
        cost_estimate=pl.CostEstimate(
            flops=8 * sources * text_rows * depth * columns, bytes_accessed=4 * MIB, transcendentals=0
        ),
        name="project",
    )(spot, received, *weights)


def cross_kernel(length_ref, spot_ref, q_ref, c_ref, near_ref, far_ref, out_ref, keep_ref, give_ref, total_ref):
    step = pl.program_id(0)
    block = out_ref.shape[0]
    tokens = near_ref.shape[0]
    q = q_ref[...].reshape(block, HD)
    cot = c_ref[...].reshape(block, HD)
    text_kv = (near_ref[...] + far_ref[...]).astype(jnp.bfloat16)
    text_keys = text_kv[:, :HD]
    text_vals = text_kv[:, HD:]
    live = lax.broadcasted_iota(jnp.int32, (tokens, 1), 0) < length_ref[0]
    scores = lax.dot_general(text_keys, q, NT, preferred_element_type=jnp.float32) * SCALE
    scores = jnp.where(live, scores, -jnp.inf)
    top = jnp.max(scores, axis=0, keepdims=True)
    expo = jnp.exp(scores - top)
    soft = expo / jnp.sum(expo, axis=0, keepdims=True)
    soft_low = soft.astype(jnp.bfloat16)
    out_t = lax.dot_general(text_vals, soft_low, TN, preferred_element_type=jnp.float32)
    out_ref[...] = out_t.T
    back = lax.dot_general(text_vals, cot, NT, preferred_element_type=jnp.float32)
    inner = jnp.sum(soft * back, axis=0, keepdims=True)
    grad_scores = (soft * (back - inner) * SCALE).astype(jnp.bfloat16)
    grad_keys = jnp.dot(grad_scores, q, preferred_element_type=jnp.float32)
    grad_vals = jnp.dot(soft_low, cot, preferred_element_type=jnp.float32)

    grads = jnp.concatenate([grad_keys, grad_vals], axis=1).reshape(total_ref.shape)

    @pl.when(step == 0)
    def _():
        total_ref[...] = grads

    @pl.when(step > 0)
    def _():
        total_ref[...] += grads

    @pl.when(step == pl.num_programs(0) - 1)
    def _():
        core = spot_ref[2]
        keep_ref[...] = total_ref[:, core].reshape(keep_ref.shape)
        give_ref[...] = total_ref[:, 1 - core].reshape(give_ref.shape)


def cross_attend(length, spot, received, rows, near, far, blocks=2):
    sources, pieces, _ = received.shape
    queries = sources * rows
    tokens, columns = near.shape
    last = pieces // rows
    text = pl.BlockSpec((tokens, columns), lambda j, n, s: (0, 0))
    half = pl.BlockSpec((tokens // 2, columns), lambda j, n, s: (0, 0))
    return pl.pallas_call(
        cross_kernel,
        grid_spec=pltpu.PrefetchScalarGridSpec(
            num_scalar_prefetch=2,
            grid=(blocks,),
            in_specs=[
                pl.BlockSpec((sources // blocks, rows, HD), lambda j, n, s: (j, last - 2, 0)),
                pl.BlockSpec((sources // blocks, rows, HD), lambda j, n, s: (j, last - 1, 0)),
                text,
                text,
            ],
            out_specs=[pl.BlockSpec((queries // blocks, HD), lambda j, n, s: (j, 0)), half, half],
            scratch_shapes=[pltpu.VMEM((sources // 2, 2, tokens // sources, columns), jnp.float32)],
        ),
        out_shape=[
            jax.ShapeDtypeStruct((queries, HD), jnp.float32),
            jax.ShapeDtypeStruct((tokens // 2, columns), jnp.float32),
            jax.ShapeDtypeStruct((tokens // 2, columns), jnp.float32),
        ],
        compiler_params=pltpu.CompilerParams(vmem_limit_bytes=56 * MIB),
        cost_estimate=pl.CostEstimate(
            flops=10 * queries * tokens * HD, bytes_accessed=4 * MIB, transcendentals=queries * tokens
        ),
        name="cross",
    )(length, spot, received, received, near, far)


def self_kernel(q_ref, near_ref, far_ref, cross_ref, out_ref):
    block = out_ref.shape[0]
    half = near_ref.shape[0] * near_ref.shape[2]
    q = q_ref[...].reshape(block, HD)
    scores = [
        lax.dot_general(q, ref[:, 0].reshape(half, HD), NT, preferred_element_type=jnp.float32)
        for ref in (near_ref, far_ref)
    ]
    top = jnp.maximum(*[jnp.max(s, axis=1, keepdims=True) for s in scores])
    total = 0.0
    out = 0.0
    for s, ref in zip(scores, (near_ref, far_ref)):
        expo = jnp.exp2((s - top) * (SCALE * LOG2E))
        total += jnp.sum(expo, axis=1, keepdims=True)
        out += jnp.dot(
            expo.astype(jnp.bfloat16), ref[:, 1].reshape(half, HD), preferred_element_type=jnp.float32
        )
    out_ref[...] = (out / total + cross_ref[...]).astype(out_ref.dtype)


def self_attend(received, near, far, cross_out, blocks=8):
    sources, _, rows, _ = near.shape
    queries = sources * rows
    last = received.shape[1] // rows
    whole = pl.BlockSpec(near.shape, lambda j: (0, 0, 0, 0))
    return pl.pallas_call(
        self_kernel,
        grid=(blocks,),
        in_specs=[
            pl.BlockSpec((sources // blocks, rows, HD), lambda j: (j, last - 2, 0)),
            whole,
            whole,
            pl.BlockSpec((queries // blocks, HD), lambda j: (j, 0)),
        ],
        out_specs=pl.BlockSpec((queries // blocks, HD), lambda j: (j, 0)),
        out_shape=jax.ShapeDtypeStruct((queries, HD), jnp.bfloat16),
        compiler_params=pltpu.CompilerParams(vmem_limit_bytes=20 * MIB),
        cost_estimate=pl.CostEstimate(
            flops=8 * queries * queries * HD, bytes_accessed=5 * MIB, transcendentals=2 * queries * queries
        ),
        name="self_attention",
    )(received, near, far, cross_out)


def finish_kernel(spot_ref, text_any, kv_any, keep_ref, give_ref, text_ref, kv_ref, sems):
    core, home = spot_ref[2], spot_ref[3]
    n_dp = text_any.shape[1]
    tokens = kv_any.shape[1]
    wanted = lax.rem(home + core, 2)
    copies = [
        (
            pltpu.make_async_copy(text_any.at[:, sample], text_ref.at[sample], sems.at[0, sample]),
            pltpu.make_async_copy(kv_any.at[wanted * n_dp + sample], kv_ref.at[0, sample], sems.at[1, sample]),
            pltpu.make_async_copy(kv_any.at[(1 - wanted) * n_dp + sample], kv_ref.at[1, sample], sems.at[2, sample]),
        )
        for sample in range(n_dp)
    ]
    for group in copies:
        for copy in group:
            copy.start()
    keep, give = 0.0, 0.0
    for sample, group in enumerate(copies):
        for copy in group:
            copy.wait()
        text = text_ref[sample].reshape(tokens, text_any.shape[3])
        keep += lax.dot_general(text, kv_ref[0, sample], TN, preferred_element_type=jnp.float32)
        give += lax.dot_general(text, kv_ref[1, sample], TN, preferred_element_type=jnp.float32)
    keep_ref[...] = keep
    give_ref[...] = give


def finish(spot, text, kv_all):
    chips, n_dp, text_rows, depth = text.shape
    _, tokens, columns = kv_all.shape
    vmem = pl.BlockSpec(memory_space=pltpu.VMEM)
    hbm = pl.BlockSpec(memory_space=pltpu.HBM)
    return pl.pallas_call(
        finish_kernel,
        in_specs=[pl.BlockSpec(memory_space=pltpu.SMEM), hbm, hbm],
        out_specs=[vmem, vmem],
        out_shape=[jax.ShapeDtypeStruct((depth, columns), jnp.float32)] * 2,
        scratch_shapes=[
            pltpu.VMEM((n_dp, chips, text_rows, depth), text.dtype),
            pltpu.VMEM((2, n_dp, tokens, columns), kv_all.dtype),
            pltpu.SemaphoreType.DMA((3, n_dp)),
        ],
        compiler_params=pltpu.CompilerParams(vmem_limit_bytes=56 * MIB),
        cost_estimate=pl.CostEstimate(flops=4 * text.size * columns, bytes_accessed=6 * MIB, transcendentals=0),
        name="finish",
    )(spot, text, kv_all)


def local(queries, keys, values, cotangent, captions, caption_len, proj_weight):
    side, turn, core = lax.axis_index("g"), lax.axis_index("d"), lax.axis_index("c")
    sides, n_dp = lax.axis_size("g"), lax.axis_size("d")
    n_ring = sides * n_dp
    n_chips = lax.axis_size("y") * lax.axis_size("x")
    home_side = lax.axis_index("y") // (lax.axis_size("y") // 2)
    spot = jnp.stack([side, turn, core, home_side]).astype(jnp.int32)
    text_rows, features = captions.shape[1:]

    def across(chip):
        return (chip + n_chips // 2) % n_chips

    passed = lax.ppermute(
        proj_weight,
        PLANE,
        [(2 * j, 2 * j + 1) for j in range(n_chips)] + [(2 * j + 1, 2 * across(j)) for j in range(n_chips)],
    )
    second = lax.ppermute(proj_weight, PLANE, [(2 * j + 1, 2 * across(j) + 1) for j in range(n_chips)])
    sent, blocks = prepare(spot, queries, cotangent, captions, n_dp)

    sent, passed, second = lax.optimization_barrier((sent, passed, second))
    received = lax.all_to_all(sent, PLANE, 0, 0, tiled=True)
    at_home = jnp.where(core == 0, proj_weight, passed)
    away = jnp.where(core == 0, passed, second)
    head_of_side = (jnp.where(home_side == 0, at_home, away), jnp.where(home_side == 0, away, at_home))

    def place(z, c):
        g, d = divmod(z % n_ring, n_dp)
        return (g * sides + c) * n_dp + d

    def block_for(distance):
        to_side = (side * n_dp + turn + distance + n_ring) % n_ring // n_dp
        return jnp.where(to_side == 0, head_of_side[0], head_of_side[1])

    def send(block, up, down):
        pairs = [(place(z, 0), place(z + up, 0)) for z in range(n_ring) if up]
        pairs += [(place(z, 1), place(z + down, 1)) for z in range(n_ring)]
        return lax.ppermute(block, ("g", "c", "d"), pairs)

    reach = n_dp // 2
    weights = [jnp.where(side == 0, head_of_side[0], head_of_side[1])]
    weights += [send(block_for((1 - 2 * core) * t), t, -t) for t in range(1, reach)]
    weights.append(send(block_for(-reach)[:, :HD], 0, -reach))
    weights.append(send(block_for(reach)[:, HD:], 0, reach))

    received, keys, values = lax.optimization_barrier((received, keys, values))
    near = lax.all_to_all(pack(spot, keys, values), PLANE, 0, 0, tiled=True)

    text_near = project(spot, received, text_rows, weights)
    text_far = lax.ppermute(text_near, "c", SWAP)
    rows = queries.shape[1] // 2
    cross_out, keep, give = cross_attend(caption_len, spot, received, rows, text_near, text_far)

    kv_half = (keep + lax.ppermute(give, "c", SWAP)).astype(jnp.bfloat16)
    kv_half, near, blocks = lax.optimization_barrier((kv_half, near, blocks))

    kv_all = lax.all_gather(kv_half, RING, axis=0, tiled=False)

    by_sample = lax.all_to_all(blocks, "d", 0, 0, tiled=True)
    spread = lax.all_to_all(
        jnp.broadcast_to(by_sample[None], (n_chips,) + by_sample.shape), ("y", "x"), 0, 0, tiled=True
    )

    far = lax.ppermute(near, "c", SWAP)
    out_rows = self_attend(received, near, far, cross_out)
    spread, out_rows = lax.optimization_barrier((spread, out_rows))
    back = lax.all_to_all(out_rows.reshape(near.shape[0], rows, HD), PLANE, 0, 0, tiled=True)
    attended = unpack(spot, back)

    spread, back = lax.optimization_barrier((spread, back))
    keep, give = finish(spot, spread, kv_all)
    total = keep + lax.ppermute(give, "c", SWAP)
    moved = lax.ppermute(
        total.astype(jnp.bfloat16), PLANE, [(2 * j + 1, 2 * across(j) + 1) for j in range(n_chips)]
    )
    proj_grad = jnp.where(core == 0, total, moved.astype(jnp.float32))
    return attended, proj_grad


def solution(mesh):
    inner = Mesh(mesh.devices.reshape(2, 4, 4, 2, 8), ("g", "y", "x", "c", "d"))
    return jax.shard_map(
        local,
        mesh=inner,
        in_specs=(
            P("d", PLANE, None),
            P("d", PLANE, None),
            P("d", PLANE, "g"),
            P("d", PLANE, "g"),
            P("d", PLANE, None),
            P("d"),
            P("d", PLANE),
        ),
        out_specs=(P("d", PLANE, "g"), P("d", PLANE)),
        check_vma=False,
    )
```

```python
import math

import jax
import jax.numpy as jnp
from jax import lax
from jax.experimental import pallas as pl
from jax.experimental.pallas import tpu as pltpu
from jax.sharding import Mesh
from jax.sharding import PartitionSpec as P

HD = 128
SCALE = 1.0 / math.sqrt(HD)
LOG2E = math.log2(math.e)
PLANE = ("y", "x", "c")
RING = ("g", "d")
NT = (((1,), (1,)), ((), ()))
TN = (((0,), (0,)), ((), ()))
MIB = 1024 * 1024
SWAP = [(0, 1), (1, 0)]


def mirrored(chip, chips, width=4):
    return chips - width - chip + 2 * (chip % width)


def column_of(chip, chips, side):
    half = chips // 2
    first = 2 * (chip % half)
    second = 2 * (mirrored(chip, chips) % half) + 1
    return pl.multiple_of(jnp.where(side == chip // half, first, second) * HD, HD)


def prepare_kernel(
    spot_ref, wide_any, half_any, text_any, out_ref, blocks_ref, wide_ref, half_ref, text_ref, normed_ref, sems
):
    here = spot_ref[1]
    dests = out_ref.shape[0]
    width = half_any.shape[2]
    columns = pl.ds(pl.multiple_of(spot_ref[0] * width, width), width)
    copies = [
        pltpu.make_async_copy(text_any, text_ref, sems.at[0]),
        pltpu.make_async_copy(wide_any.at[:, :, columns], wide_ref, sems.at[1]),
        pltpu.make_async_copy(half_any, half_ref, sems.at[2]),
    ]
    for copy in copies:
        copy.start()
    copies[0].wait()
    n_dp, text_rows, depth = blocks_ref.shape
    rows = half_ref.shape[1] // 2
    wide = text_ref[0].astype(jnp.float32)
    square = jnp.mean(wide * wide, axis=-1, keepdims=True)
    normed_ref[...] = (wide * lax.rsqrt(square + 1e-06)).astype(jnp.bfloat16)
    for block in range(n_dp):
        blocks_ref[block] = normed_ref[:, block * depth : (block + 1) * depth]
    copies[1].wait()
    copies[2].wait()
    slots = n_dp // 2
    start = slots * depth // HD * text_rows
    for part in range(2):
        for slot in range(slots):
            away = (slot or slots) if part else -slot
            block = lax.rem(here + away + n_dp, n_dp)
            for lane in range(depth // HD):
                column = pl.multiple_of(block * depth + lane * HD, HD)
                piece = normed_ref[:, pl.ds(column, HD)]
                place = (slot * (depth // HD) + lane) * text_rows
                for head in range(dests // 2):
                    out_ref[2 * head + part, place : place + text_rows] = piece
        for head in range(dests // 2):
            columns = pl.ds(column_of(head, dests // 2, spot_ref[0]), HD)
            for slot, ref in enumerate((wide_ref, half_ref)):
                out_ref[2 * head + part, start + slot * rows : start + (slot + 1) * rows] = ref[
                    0, part * rows : (part + 1) * rows, columns
                ]


def prepare(spot, wide, half, text, n_dp):
    _, rows, width = half.shape
    _, text_rows, features = text.shape
    dests = 2 * width // HD
    pieces = features // 2 // HD * text_rows + rows
    depth = features // n_dp
    return pl.pallas_call(
        prepare_kernel,
        grid_spec=pltpu.PrefetchScalarGridSpec(
            num_scalar_prefetch=1,
            grid=(1,),
            in_specs=[pl.BlockSpec(memory_space=pltpu.HBM)] * 3,
            out_specs=[
                pl.BlockSpec((dests, pieces, HD), lambda j, spot_ref: (0, 0, 0)),
                pl.BlockSpec((n_dp, text_rows, depth), lambda j, spot_ref: (0, 0, 0)),
            ],
            scratch_shapes=[
                pltpu.VMEM(half.shape, half.dtype),
                pltpu.VMEM(half.shape, half.dtype),
                pltpu.VMEM(text.shape, text.dtype),
                pltpu.VMEM((text_rows, features), jnp.bfloat16),
                pltpu.SemaphoreType.DMA((3,)),
            ],
        ),
        out_shape=[
            jax.ShapeDtypeStruct((dests, pieces, HD), half.dtype),
            jax.ShapeDtypeStruct((n_dp, text_rows, depth), half.dtype),
        ],
        compiler_params=pltpu.CompilerParams(vmem_limit_bytes=12 * MIB),
        cost_estimate=pl.CostEstimate(
            flops=4 * text.size, bytes_accessed=2 * dests * pieces * HD + 4 * rows * width, transcendentals=0
        ),
        name="prepare",
    )(spot, wide, half, text)


def pack_kernel(spot_ref, wide_ref, half_ref, out_ref):
    rows = out_ref.shape[2]
    for dest in range(out_ref.shape[0]):
        head, part = dest // 2, dest % 2
        columns = pl.ds(column_of(head, out_ref.shape[0] // 2, spot_ref[0]), HD)
        for slot, ref in enumerate((wide_ref, half_ref)):
            out_ref[dest, slot] = ref[0, part * rows : (part + 1) * rows, columns]


def pack(spot, wide, half):
    _, rows, width = half.shape
    dests = 2 * width // HD
    return pl.pallas_call(
        pack_kernel,
        grid_spec=pltpu.PrefetchScalarGridSpec(
            num_scalar_prefetch=1,
            grid=(1,),
            in_specs=[
                pl.BlockSpec((1, rows, width), lambda j, spot_ref: (0, 0, spot_ref[0])),
                pl.BlockSpec((1, rows, width), lambda j, spot_ref: (0, 0, 0)),
            ],
            out_specs=pl.BlockSpec((dests, 2, rows // 2, HD), lambda j, spot_ref: (0, 0, 0, 0)),
        ),
        out_shape=jax.ShapeDtypeStruct((dests, 2, rows // 2, HD), half.dtype),
        compiler_params=pltpu.CompilerParams(vmem_limit_bytes=8 * MIB),
        cost_estimate=pl.CostEstimate(flops=0, bytes_accessed=4 * rows * width * 2, transcendentals=0),
        name="pack",
    )(spot, wide, half)


def unpack_kernel(spot_ref, in_ref, out_ref):
    rows = in_ref.shape[1]
    for source in range(in_ref.shape[0]):
        head, part = source // 2, source % 2
        columns = pl.ds(column_of(head, in_ref.shape[0] // 2, spot_ref[0]), HD)
        out_ref[0, part * rows : (part + 1) * rows, columns] = in_ref[source]


def unpack(spot, pieces):
    sources, rows, _ = pieces.shape
    width = sources // 2 * HD
    return pl.pallas_call(
        unpack_kernel,
        in_specs=[pl.BlockSpec(memory_space=pltpu.SMEM), pl.BlockSpec(memory_space=pltpu.VMEM)],
        out_shape=jax.ShapeDtypeStruct((1, 2 * rows, width), pieces.dtype),
        compiler_params=pltpu.CompilerParams(vmem_limit_bytes=4 * MIB),
        cost_estimate=pl.CostEstimate(flops=0, bytes_accessed=8 * rows * width, transcendentals=0),
        name="unpack",
    )(spot, pieces)


def project_kernel(spot_ref, text_ref, *refs):
    weight_refs, (out_ref, full_ref, half_ref, sems) = refs[:6], refs[6:]
    depth = full_ref.shape[1]
    groups = depth // HD
    sources = text_ref.shape[0]
    rows = out_ref.shape[0] // sources
    slots = [full_ref.at[k] for k in range(4)] + [half_ref.at[k] for k in range(2)]
    copies = [
        pltpu.make_async_copy(source, slot, sems.at[k])
        for k, (source, slot) in enumerate(zip(weight_refs, slots))
    ]
    for copy in copies:
        copy.start()
    for copy in copies:
        copy.wait()
    far = jnp.concatenate([half_ref[0], half_ref[1]], axis=1)
    weights = [jnp.where(spot_ref[2] == 0, full_ref[0], far), full_ref[1], full_ref[2], full_ref[3]]
    total = 0.0
    for slot, weight in enumerate(weights):
        block = jnp.concatenate(
            [
                text_ref[:, (slot * groups + k) * rows : (slot * groups + k + 1) * rows].reshape(sources * rows, HD)
                for k in range(groups)
            ],
            axis=1,
        )
        total += jnp.dot(block, weight, preferred_element_type=jnp.float32)
    out_ref[...] = total


def project(spot, received, text_rows, weights):
    sources = received.shape[0]
    depth, columns = weights[0].shape
    pieces = 4 * depth // HD * text_rows
    return pl.pallas_call(
        project_kernel,
        grid=(1,),
        in_specs=[
            pl.BlockSpec(memory_space=pltpu.SMEM),
            pl.BlockSpec((sources, pieces, HD), lambda j: (0, 0, 0)),
            *[pl.BlockSpec(memory_space=pltpu.HBM)] * 6,
        ],
        out_specs=pl.BlockSpec((sources * text_rows, columns), lambda j: (0, 0)),
        out_shape=jax.ShapeDtypeStruct((sources * text_rows, columns), jnp.float32),
        scratch_shapes=[
            pltpu.VMEM((4, depth, columns), jnp.bfloat16),
            pltpu.VMEM((2, depth, columns // 2), jnp.bfloat16),
            pltpu.SemaphoreType.DMA((6,)),
        ],
        compiler_params=pltpu.CompilerParams(vmem_limit_bytes=10 * MIB),
        cost_estimate=pl.CostEstimate(
            flops=8 * sources * text_rows * depth * columns, bytes_accessed=4 * MIB, transcendentals=0
        ),
        name="project",
    )(spot, received, *weights)


def cross_kernel(length_ref, spot_ref, q_ref, c_ref, near_ref, far_ref, out_ref, keep_ref, give_ref, total_ref):
    step = pl.program_id(0)
    block = out_ref.shape[0]
    tokens = near_ref.shape[0]
    q = q_ref[...].reshape(block, HD)
    cot = c_ref[...].reshape(block, HD)
    text_kv = (near_ref[...] + far_ref[...]).astype(jnp.bfloat16)
    text_keys = text_kv[:, :HD]
    text_vals = text_kv[:, HD:]
    live = lax.broadcasted_iota(jnp.int32, (tokens, 1), 0) < length_ref[0]
    scores = lax.dot_general(text_keys, q, NT, preferred_element_type=jnp.float32) * SCALE
    scores = jnp.where(live, scores, -jnp.inf)
    top = jnp.max(scores, axis=0, keepdims=True)
    expo = jnp.exp(scores - top)
    soft = expo / jnp.sum(expo, axis=0, keepdims=True)
    soft_low = soft.astype(jnp.bfloat16)
    out_t = lax.dot_general(text_vals, soft_low, TN, preferred_element_type=jnp.float32)
    out_ref[...] = out_t.T
    back = lax.dot_general(text_vals, cot, NT, preferred_element_type=jnp.float32)
    inner = jnp.sum(soft * back, axis=0, keepdims=True)
    grad_scores = (soft * (back - inner) * SCALE).astype(jnp.bfloat16)
    grad_keys = jnp.dot(grad_scores, q, preferred_element_type=jnp.float32)
    grad_vals = jnp.dot(soft_low, cot, preferred_element_type=jnp.float32)

    grads = jnp.concatenate([grad_keys, grad_vals], axis=1).reshape(total_ref.shape)

    @pl.when(step == 0)
    def _():
        total_ref[...] = grads

    @pl.when(step > 0)
    def _():
        total_ref[...] += grads

    @pl.when(step == pl.num_programs(0) - 1)
    def _():
        core = spot_ref[2]
        keep_ref[...] = total_ref[:, core].reshape(keep_ref.shape)
        give_ref[...] = total_ref[:, 1 - core].reshape(give_ref.shape)


def cross_attend(length, spot, received, rows, near, far, blocks=2):
    sources, pieces, _ = received.shape
    queries = sources * rows
    tokens, columns = near.shape
    last = pieces // rows
    text = pl.BlockSpec((tokens, columns), lambda j, n, s: (0, 0))
    half = pl.BlockSpec((tokens // 2, columns), lambda j, n, s: (0, 0))
    return pl.pallas_call(
        cross_kernel,
        grid_spec=pltpu.PrefetchScalarGridSpec(
            num_scalar_prefetch=2,
            grid=(blocks,),
            in_specs=[
                pl.BlockSpec((sources // blocks, rows, HD), lambda j, n, s: (j, last - 2, 0)),
                pl.BlockSpec((sources // blocks, rows, HD), lambda j, n, s: (j, last - 1, 0)),
                text,
                text,
            ],
            out_specs=[pl.BlockSpec((queries // blocks, HD), lambda j, n, s: (j, 0)), half, half],
            scratch_shapes=[pltpu.VMEM((sources // 2, 2, tokens // sources, columns), jnp.float32)],
        ),
        out_shape=[
            jax.ShapeDtypeStruct((queries, HD), jnp.float32),
            jax.ShapeDtypeStruct((tokens // 2, columns), jnp.float32),
            jax.ShapeDtypeStruct((tokens // 2, columns), jnp.float32),
        ],
        compiler_params=pltpu.CompilerParams(vmem_limit_bytes=56 * MIB),
        cost_estimate=pl.CostEstimate(
            flops=10 * queries * tokens * HD, bytes_accessed=4 * MIB, transcendentals=queries * tokens
        ),
        name="cross",
    )(length, spot, received, received, near, far)


def self_kernel(q_ref, near_ref, far_ref, cross_ref, out_ref):
    block = out_ref.shape[0]
    half = near_ref.shape[0] * near_ref.shape[2]
    q = q_ref[...].reshape(block, HD)
    scores = [
        lax.dot_general(q, ref[:, 0].reshape(half, HD), NT, preferred_element_type=jnp.float32)
        for ref in (near_ref, far_ref)
    ]
    top = jnp.maximum(*[jnp.max(s, axis=1, keepdims=True) for s in scores])
    total = 0.0
    out = 0.0
    for s, ref in zip(scores, (near_ref, far_ref)):
        expo = jnp.exp2((s - top) * (SCALE * LOG2E))
        total += jnp.sum(expo, axis=1, keepdims=True)
        out += jnp.dot(
            expo.astype(jnp.bfloat16), ref[:, 1].reshape(half, HD), preferred_element_type=jnp.float32
        )
    out_ref[...] = (out / total + cross_ref[...]).astype(out_ref.dtype)


def self_attend(received, near, far, cross_out, blocks=8):
    sources, _, rows, _ = near.shape
    queries = sources * rows
    last = received.shape[1] // rows
    whole = pl.BlockSpec(near.shape, lambda j: (0, 0, 0, 0))
    return pl.pallas_call(
        self_kernel,
        grid=(blocks,),
        in_specs=[
            pl.BlockSpec((sources // blocks, rows, HD), lambda j: (j, last - 2, 0)),
            whole,
            whole,
            pl.BlockSpec((queries // blocks, HD), lambda j: (j, 0)),
        ],
        out_specs=pl.BlockSpec((queries // blocks, HD), lambda j: (j, 0)),
        out_shape=jax.ShapeDtypeStruct((queries, HD), jnp.bfloat16),
        compiler_params=pltpu.CompilerParams(vmem_limit_bytes=56 * MIB),
        cost_estimate=pl.CostEstimate(
            flops=8 * queries * queries * HD, bytes_accessed=5 * MIB, transcendentals=2 * queries * queries
        ),
        name="self_attention",
    )(received, near, far, cross_out)


def finish_kernel(spot_ref, text_any, kv_any, keep_ref, give_ref, text_ref, kv_ref, sems):
    core, home = spot_ref[2], spot_ref[3]
    n_dp = text_any.shape[1]
    tokens = kv_any.shape[1]
    wanted = lax.rem(home + core, 2)
    copies = [
        (
            pltpu.make_async_copy(text_any.at[:, sample], text_ref.at[sample], sems.at[0, sample]),
            pltpu.make_async_copy(kv_any.at[wanted * n_dp + sample], kv_ref.at[0, sample], sems.at[1, sample]),
            pltpu.make_async_copy(kv_any.at[(1 - wanted) * n_dp + sample], kv_ref.at[1, sample], sems.at[2, sample]),
        )
        for sample in range(n_dp)
    ]
    for group in copies:
        for copy in group:
            copy.start()
    keep, give = 0.0, 0.0
    for sample, group in enumerate(copies):
        for copy in group:
            copy.wait()
        text = text_ref[sample].reshape(tokens, text_any.shape[3])
        keep += lax.dot_general(text, kv_ref[0, sample], TN, preferred_element_type=jnp.float32)
        give += lax.dot_general(text, kv_ref[1, sample], TN, preferred_element_type=jnp.float32)
    keep_ref[...] = keep
    give_ref[...] = give


def finish(spot, text, kv_all):
    chips, n_dp, text_rows, depth = text.shape
    _, tokens, columns = kv_all.shape
    vmem = pl.BlockSpec(memory_space=pltpu.VMEM)
    hbm = pl.BlockSpec(memory_space=pltpu.HBM)
    return pl.pallas_call(
        finish_kernel,
        in_specs=[pl.BlockSpec(memory_space=pltpu.SMEM), hbm, hbm],
        out_specs=[vmem, vmem],
        out_shape=[jax.ShapeDtypeStruct((depth, columns), jnp.float32)] * 2,
        scratch_shapes=[
            pltpu.VMEM((n_dp, chips, text_rows, depth), text.dtype),
            pltpu.VMEM((2, n_dp, tokens, columns), kv_all.dtype),
            pltpu.SemaphoreType.DMA((3, n_dp)),
        ],
        compiler_params=pltpu.CompilerParams(vmem_limit_bytes=56 * MIB),
        cost_estimate=pl.CostEstimate(flops=4 * text.size * columns, bytes_accessed=6 * MIB, transcendentals=0),
        name="finish",
    )(spot, text, kv_all)


def local(queries, keys, values, cotangent, captions, caption_len, proj_weight):
    side, turn, core = lax.axis_index("g"), lax.axis_index("d"), lax.axis_index("c")
    sides, n_dp = lax.axis_size("g"), lax.axis_size("d")
    n_ring = sides * n_dp
    n_chips = lax.axis_size("y") * lax.axis_size("x")
    home_side = lax.axis_index("y") // (lax.axis_size("y") // 2)
    spot = jnp.stack([side, turn, core, home_side]).astype(jnp.int32)
    text_rows, features = captions.shape[1:]

    def across(chip):
        return mirrored(chip, n_chips, lax.axis_size("x"))

    passed = lax.ppermute(
        proj_weight,
        PLANE,
        [(2 * j, 2 * j + 1) for j in range(n_chips)] + [(2 * j + 1, 2 * across(j)) for j in range(n_chips)],
    )
    second = lax.ppermute(proj_weight, PLANE, [(2 * j + 1, 2 * across(j) + 1) for j in range(n_chips)])
    sent, blocks = prepare(spot, queries, cotangent, captions, n_dp)

    sent, passed, second = lax.optimization_barrier((sent, passed, second))
    received = lax.all_to_all(sent, PLANE, 0, 0, tiled=True)
    at_home = jnp.where(core == 0, proj_weight, passed)
    away = jnp.where(core == 0, passed, second)
    head_of_side = (jnp.where(home_side == 0, at_home, away), jnp.where(home_side == 0, away, at_home))

    def place(z, c):
        g, d = divmod(z % n_ring, n_dp)
        return (g * sides + c) * n_dp + d

    def block_for(distance):
        to_side = (side * n_dp + turn + distance + n_ring) % n_ring // n_dp
        return jnp.where(to_side == 0, head_of_side[0], head_of_side[1])

    def send(block, up, down):
        pairs = [(place(z, 0), place(z + up, 0)) for z in range(n_ring) if up]
        pairs += [(place(z, 1), place(z + down, 1)) for z in range(n_ring)]
        return lax.ppermute(block, ("g", "c", "d"), pairs)

    reach = n_dp // 2
    weights = [jnp.where(side == 0, head_of_side[0], head_of_side[1])]
    weights += [send(block_for((1 - 2 * core) * t), t, -t) for t in range(1, reach)]
    weights.append(send(block_for(-reach)[:, :HD], 0, -reach))
    weights.append(send(block_for(reach)[:, HD:], 0, reach))

    received, keys, values = lax.optimization_barrier((received, keys, values))
    near = lax.all_to_all(pack(spot, keys, values), PLANE, 0, 0, tiled=True)

    text_near = project(spot, received, text_rows, weights)
    text_far = lax.ppermute(text_near, "c", SWAP)
    rows = queries.shape[1] // 2
    cross_out, keep, give = cross_attend(caption_len, spot, received, rows, text_near, text_far)

    kv_half = (keep + lax.ppermute(give, "c", SWAP)).astype(jnp.bfloat16)
    kv_half, near, blocks = lax.optimization_barrier((kv_half, near, blocks))

    kv_all = lax.all_gather(kv_half, RING, axis=0, tiled=False)

    by_sample = lax.all_to_all(blocks, "d", 0, 0, tiled=True)
    spread = lax.all_to_all(
        jnp.broadcast_to(by_sample[None], (n_chips,) + by_sample.shape), ("y", "x"), 0, 0, tiled=True
    )

    far = lax.ppermute(near, "c", SWAP)
    out_rows = self_attend(received, near, far, cross_out)
    spread, out_rows = lax.optimization_barrier((spread, out_rows))
    back = lax.all_to_all(out_rows.reshape(near.shape[0], rows, HD), PLANE, 0, 0, tiled=True)
    attended = unpack(spot, back)

    spread, back = lax.optimization_barrier((spread, back))
    keep, give = finish(spot, spread, kv_all)
    total = keep + lax.ppermute(give, "c", SWAP)
    moved = lax.ppermute(
        total.astype(jnp.bfloat16), PLANE, [(2 * j + 1, 2 * across(j) + 1) for j in range(n_chips)]
    )
    proj_grad = jnp.where(core == 0, total, moved.astype(jnp.float32))
    return attended, proj_grad


def solution(mesh):
    inner = Mesh(mesh.devices.reshape(2, 4, 4, 2, 8), ("g", "y", "x", "c", "d"))
    return jax.shard_map(
        local,
        mesh=inner,
        in_specs=(
            P("d", PLANE, None),
            P("d", PLANE, None),
            P("d", PLANE, "g"),
            P("d", PLANE, "g"),
            P("d", PLANE, None),
            P("d"),
            P("d", PLANE),
        ),
        out_specs=(P("d", PLANE, "g"), P("d", PLANE)),
        check_vma=False,
    )
```
